512 devices in a mesh: group: 32 (over z_lo, x), module: 16 (over z_hi, y, core).
Axes of the slice: x: 4, y: 4, z: 16 (z_hi: 2, z_lo: 8; z = z_hi * 8 + z_lo), core: 2. Of those that a mesh axis runs over, the one named last changes fastest.
Arguments:
- train_grads: bfloat16 [32768, 16, 1024], P(('group', 'module')), may hold values from -6 to 6
- query_grads: bfloat16 [32, 32, 16, 1024], P('group', None, 'module'), may hold values from -6 to 6
- basis_out: bfloat16 [16, 32, 32], P('module'), may hold values from -1 to 1
- basis_in: bfloat16 [16, 32, 32], P('module'), may hold values from -1 to 1
- eigenvalues: float32 [16, 1024], P('module'), may hold values from 0.05 to 5
- owner_groups: int32 [4], replicated, may hold values from 0 to 31, as said below
- module_order: int32 [16], replicated, may hold values from 0 to 15, each once
Outputs:
- scores: float32 [32768, 128], P(('group', 'module'))
The draws below stay inside these ranges and needn't reach their ends.
Inputs may be any that keep to these rules, and one draw needn't show every extreme that they name: `owner_groups`: 4 different groups, the first and the last group among them. `module_order`: each module exactly once.
All inputs are finite; a program needn't handle non-finite values.
Results may differ from the reference program's by a relative error of at most 0.0037.
Values may be sent and summed in bfloat16 or wider, within the bound.
A program may use at most 64 MiB of HBM per device.

```python
import math
import jax
import jax.numpy as jnp
from jax import lax

SIDE = 32
W = 1024
MODULES = 16
EXAMPLES = 32768
QPO = 32
OWNERS = 4
QUERIES = 128
N_GROUP = 32


def draw_owner_groups(key, part):
    middle = jax.random.permutation(jax.random.fold_in(key, 11), N_GROUP - 2)[:OWNERS - 2] + 1
    joined = jnp.concatenate([jnp.zeros((1,), jnp.int32), middle.astype(jnp.int32), jnp.full((1,), N_GROUP - 1, jnp.int32)])
    shuffle = jax.random.permutation(jax.random.fold_in(key, 12), OWNERS)
    return joined[shuffle].astype(jnp.int32)


def level_of(own_key, extent, cuts, least, high):
    def one(axis_at, blocks):
        draws = jax.random.uniform(jax.random.fold_in(jax.random.fold_in(own_key, 6), axis_at), (blocks,), jnp.float32, least / len(cuts), high / len(cuts))
        return jnp.repeat(jnp.exp(draws), extent[axis_at] // blocks).reshape((-1,) + (1,) * (len(extent) - axis_at - 1))

    loudness = one(*cuts[0])
    for cut in cuts[1:]:
        loudness = loudness * one(*cut)
    return loudness


def centred(rng, shape, width, most, shards=(), kind=jnp.bfloat16):
    entries = width * jax.random.normal(rng, shape, jnp.float32)
    if shards:
        entries = entries * level_of(rng, shape, shards, -0.22, 0.18)
    return jnp.clip(entries, -most, most).astype(kind)


def setup_inputs(seed: int = 0) -> dict:
    streams_of = jax.random.split(jax.random.key(seed), 8)
    return {
        "train_grads": centred(streams_of[0], (EXAMPLES, MODULES, W), 1.0, 6.0, ((0, 512),)),
        "query_grads": centred(streams_of[1], (N_GROUP, QPO, MODULES, W), 1.0, 6.0, ((0, 32), (2, 16))),
        "basis_out": centred(streams_of[2], (MODULES, SIDE, SIDE), SIDE ** -0.5, 1.0, ((0, 16),)),
        "basis_in": centred(streams_of[3], (MODULES, SIDE, SIDE), SIDE ** -0.5, 1.0, ((0, 16),)),
        "eigenvalues": jnp.clip(jnp.exp(math.log(5.0) - 4.6051702 * jax.random.uniform(streams_of[4], (MODULES, W), jnp.float32) ** level_of(streams_of[4], (MODULES, W), ((0, 16),), -0.2, 0.2)), 0.05, 5.0),
        "owner_groups": draw_owner_groups(jax.random.fold_in(streams_of[7], 71), 0),
        "module_order": jax.random.permutation(streams_of[6], MODULES).astype(jnp.int32),
    }


def build_rotator(basis_out, basis_in):
    breadth = basis_out.shape[-1]
    product = basis_out.astype(jnp.float32)[..., :, None, :, None] * basis_in.astype(jnp.float32)[..., None, :, None, :]
    return product.reshape(basis_out.shape[:-2] + (breadth * breadth, breadth * breadth)).astype(jnp.bfloat16)

def reference(train_grads, query_grads, basis_out, basis_in, eigenvalues, owner_groups, module_order):
    queries = jnp.take(query_grads, owner_groups, axis=0).reshape(QUERIES, MODULES, W)

    def add_slot(running, slot_index):
        rotator = build_rotator(basis_out[slot_index], basis_in[slot_index])
        spectrum = eigenvalues[slot_index]
        damping = 0.1 * jnp.mean(spectrum)
        column = lax.dynamic_index_in_dim(train_grads, module_order[slot_index], axis=1, keepdims=False)
        turned = jnp.dot(column, rotator, preferred_element_type=jnp.float32).astype(jnp.bfloat16)
        asked = (jnp.dot(queries[:, slot_index], rotator, preferred_element_type=jnp.float32) / (spectrum + damping)).astype(jnp.bfloat16)
        return (running + jnp.dot(turned, asked.T, preferred_element_type=jnp.float32), None)
    running = jnp.zeros((EXAMPLES, QUERIES), jnp.float32)
    running, unused = lax.scan(add_slot, running, jnp.arange(MODULES, dtype=jnp.int32))
    return running / math.sqrt(MODULES * W)
```

```python
import math

import jax
import jax.numpy as jnp
from jax import lax
from jax.sharding import PartitionSpec as P


def build_rotator(basis_out, basis_in):
    breadth = basis_out.shape[-1]
    product = (
        basis_out.astype(jnp.float32)[:, None, :, None]
        * basis_in.astype(jnp.float32)[None, :, None, :]
    )
    return product.reshape(breadth * breadth, breadth * breadth).astype(jnp.bfloat16)


def local(train_grads, query_grads, basis_out, basis_in, eigenvalues, owner_groups, module_order):
    ex_rows, modules, width = train_grads.shape
    owners, held = owner_groups.shape[0], query_grads.shape[1]
    groups = lax.axis_size("group")
    rotator = build_rotator(basis_out[0], basis_in[0])
    divisor = eigenvalues + 0.1 * jnp.mean(eigenvalues, axis=1, keepdims=True)
    owned = owner_groups == lax.axis_index("group")
    offered = jnp.where(owned[:, None, None], query_grads[0, :, 0][None], 0)
    mine = lax.psum_scatter(
        offered.reshape(owners * held, width), "group", scatter_dimension=0, tiled=True
    )
    asked = (jnp.dot(mine, rotator, preferred_element_type=jnp.float32) / divisor).astype(
        jnp.bfloat16
    )
    back = lax.dot_general(
        asked, rotator, (((1,), (1,)), ((), ())), preferred_element_type=jnp.float32
    ).astype(jnp.bfloat16)
    everywhere = lax.all_gather(back, ("group", "module"), axis=0, tiled=True)
    everywhere = everywhere.reshape(groups, modules, owners * held // groups, width)
    ordered = jnp.take(train_grads, module_order, axis=1)
    scores = jnp.einsum("esw,gsqw->egq", ordered, everywhere, preferred_element_type=jnp.float32)
    return scores.reshape(ex_rows, owners * held) * (1.0 / math.sqrt(modules * width))


def solution(mesh):
    in_specs = (
        P(("group", "module"), None, None),
        P("group", None, "module", None),
        P("module", None, None),
        P("module", None, None),
        P("module", None),
        P(),
        P(),
    )
    out_specs = P(("group", "module"), None)
    return jax.shard_map(local, mesh=mesh, in_specs=in_specs, out_specs=out_specs, check_vma=False)
```

```python
import functools
import math

import jax
import jax.numpy as jnp
from jax import lax
from jax.experimental import pallas as pl
from jax.experimental.pallas import tpu as pltpu
from jax.sharding import PartitionSpec as P

ZH, Y, C = 2, 4, 2
X = 4
F32, BF16 = jnp.float32, jnp.bfloat16


def kernel(
    dims,
    train_ref,
    query_ref,
    bout_ref,
    bin_ref,
    eig_ref,
    owner_ref,
    order_ref,
    out_ref,
    perm,
    ordered,
    gathered,
    rot,
    turned,
    bases,
    eigs,
    raw,
    offer,
    offered,
    chosen,
    asked,
    part,
    parts,
    s1s,
    s1r,
    s2s,
    s2r,
    s3s,
    s3r,
    s4s,
    s4r,
    sgs,
    sgr,
    sbs,
    sbr,
    sps,
    spr,
):
    zl_n, x_n, zh_n, y_n, c_n = dims
    t_n = y_n * c_n
    z_n = zh_n * zl_n
    rows, modules, width = train_ref.shape
    held = query_ref.shape[0]
    piece = width // zl_n
    group, module = lax.axis_index("group"), lax.axis_index("module")
    zl, xi = lax.div(group, x_n), lax.rem(group, x_n)
    zh, ti = lax.div(module, t_n), lax.rem(module, t_n)
    yi = lax.div(ti, c_n)
    zi = zh * zl_n + zl

    def at(z=None, x=None, t=None):
        z = zi if z is None else z
        x = xi if x is None else x
        t = ti if t is None else t
        return (lax.rem(z, zl_n) * x_n + x, lax.div(z, zl_n) * t_n + t)

    def remote(src, dst, send, recv, where):
        return pltpu.make_async_remote_copy(
            src_ref=src,
            dst_ref=dst,
            send_sem=send,
            recv_sem=recv,
            device_id=where,
            device_id_type=pl.DeviceIdType.MESH,
        )

    barrier = pltpu.get_barrier_semaphore()

    def greet(where):
        pl.semaphore_signal(
            barrier, inc=1, device_id=where, device_id_type=pl.DeviceIdType.MESH
        )

    @pl.loop(1, z_n)
    def _(i):
        greet(at(z=lax.rem(zi + i, z_n)))

    @pl.loop(1, x_n)
    def _(i):
        greet(at(x=lax.rem(xi + i, x_n)))

    @pl.loop(1, t_n)
    def _(i):
        greet(at(t=lax.rem(ti + i, t_n)))

    batch = 16
    span = batch * modules
    for s in range(modules):
        lane = lax.broadcasted_iota(jnp.int32, (batch, span), 1)
        row = lax.broadcasted_iota(jnp.int32, (batch, span), 0)
        hit = lane == row * modules + order_ref[s]
        perm[pl.ds(s * batch, batch), :] = jnp.where(hit, 1.0, 0.0).astype(BF16)
    for b in range(rows // batch):
        block = train_ref[pl.ds(b * batch, batch)].reshape(span, width)
        moved = jnp.dot(perm[...], block, preferred_element_type=F32).astype(BF16)
        ordered[:, pl.ds(b * batch, batch), :] = moved.reshape(modules, batch, width)

    bases[zh] = jnp.zeros(bases.shape[1:], BF16)
    bases[zh, 0, :, : bout_ref.shape[1]] = bout_ref[...]
    bases[zh, 1, :, : bin_ref.shape[1]] = bin_ref[...]
    eigs[zh] = eig_ref[...]

    pl.semaphore_wait(barrier, z_n + x_n + t_n - 3)

    def send1(z):
        return remote(
            query_ref.at[:, pl.ds(pl.multiple_of(z * piece, piece), piece)],
            raw.at[zl],
            s1s.at[z],
            s1r.at[zl],
            at(z=zh * zl_n + z),
        )

    @pl.loop(1, zl_n)
    def _(i):
        send1(lax.rem(zl + i, zl_n)).start()

    other = zh_n - 1 - zh
    twins = [
        remote(bases.at[zh], bases.at[zh], sbs.at[0], sbr.at[0], at(z=other * zl_n + zl)),
        remote(eigs.at[zh], eigs.at[zh], sbs.at[1], sbr.at[1], at(z=other * zl_n + zl)),
    ]
    for twin in twins:
        twin.start()

    def send_g(t, h):
        return remote(
            ordered.at[h * t_n + t],
            gathered.at[h, pl.ds(pl.multiple_of(ti * rows, rows), rows)],
            sgs.at[t, h],
            sgr.at[ti, h],
            at(t=t),
        )

    def got_g(t, h):
        return remote(
            ordered.at[h * t_n + t],
            gathered.at[h, pl.ds(pl.multiple_of(t * rows, rows), rows)],
            sgs.at[t, h],
            sgr.at[t, h],
            at(t=t),
        )

    @pl.loop(1, t_n)
    def _(i):
        for h in range(zh_n):
            send_g(jnp.bitwise_xor(ti, i), h).start()

    for h in range(zh_n):
        gathered[h, pl.ds(pl.multiple_of(ti * rows, rows), rows)] = ordered[h * t_n + ti]

    def build(h):
        side = bout_ref.shape[1]
        lane = lax.broadcasted_iota(jnp.int32, (bases.shape[3], width), 1)
        row = lax.broadcasted_iota(jnp.int32, (bases.shape[3], width), 0)
        wide = jnp.where(lax.div(lane, side) == row, 1.0, 0.0).astype(BF16)
        tiled = jnp.where(lax.rem(lane, side) == row, 1.0, 0.0).astype(BF16)
        outer = jnp.dot(bases[h, 0], wide, preferred_element_type=F32)
        inner = jnp.dot(bases[h, 1], tiled, preferred_element_type=F32)
        for a in range(side):
            rot[h, pl.ds(a * side, side), :] = (outer[a : a + 1] * inner).astype(BF16)

    build(zh)

    raw[zl] = query_ref[:, pl.ds(pl.multiple_of(zl * piece, piece), piece)]

    @pl.loop(1, zl_n)
    def _(i):
        z = lax.rem(zl + i, zl_n)
        remote(raw.at[z], raw.at[z], s1s.at[z], s1r.at[z], at()).wait_recv()

    for k in range(x_n):
        offer[k] = raw[lax.div(owner_ref[k], x_n)]

    def send2(x):
        return remote(offer.at[x], offered.at[xi], s2s.at[x], s2r.at[xi], at(x=x))

    @pl.loop(1, x_n)
    def _(i):
        send2(lax.rem(xi + i, x_n)).start()

    offered[xi] = offer[xi]

    @pl.loop(1, x_n)
    def _(i):
        x = lax.rem(xi + i, x_n)
        remote(offer.at[x], offered.at[x], s2s.at[x], s2r.at[x], at()).wait_recv()

    lines = pl.ds(pl.multiple_of(xi * held, held), held)
    chosen[zh, lines, pl.ds(pl.multiple_of(zl * piece, piece), piece)] = offered[
        lax.rem(owner_ref[xi], x_n)
    ]

    def chunk(z, k):
        return chosen.at[
            lax.div(z, zl_n),
            pl.ds(pl.multiple_of(k * held, held), held),
            pl.ds(pl.multiple_of(lax.rem(z, zl_n) * piece, piece), piece),
        ]

    def send3(z):
        return remote(chunk(zi, xi), chunk(zi, xi), s3s.at[z], s3r.at[zi], at(z=z))

    @pl.loop(1, z_n)
    def _(i):
        send3(lax.rem(zi + i, z_n)).start()

    for twin in twins:
        twin.wait_send()
    for i, buf in enumerate((bases, eigs)):
        remote(buf.at[other], buf.at[other], sbs.at[i], sbr.at[i], at()).wait_recv()
    build(other)

    wide_n = 256
    tiles = width // wide_n

    def turn(y):
        @pl.loop(0, zh_n * tiles)
        def _(i):
            h, n = lax.div(i, tiles), lax.rem(i, tiles)
            some = pl.ds(pl.multiple_of(y * c_n * rows, c_n * rows), c_n * rows)
            columns = pl.ds(pl.multiple_of(n * wide_n, wide_n), wide_n)
            turned[h, some, columns] = jnp.dot(
                gathered[h, some, :], rot[h, :, columns], preferred_element_type=F32
            ).astype(BF16)

    sibling = jnp.bitwise_xor(ti, 1)
    for h in range(zh_n):
        got_g(sibling, h).wait_recv()
    turn(yi)

    quarters = s4s.shape[1]
    each = z_n // quarters

    def quarter(q, k):
        per = quarters // zh_n
        return chosen.at[
            lax.div(q, per),
            pl.ds(pl.multiple_of(k * held, held), held),
            pl.ds(pl.multiple_of(lax.rem(q, per) * each * piece, each * piece), each * piece),
        ]

    def send4(x, q):
        return remote(quarter(q, xi), quarter(q, xi), s4s.at[x, q], s4r.at[xi, q], at(x=x))

    home = lax.div(zi, each)
    for j in (0, 1, quarters - 1, 2):
        q = lax.rem(home + j, quarters)

        @pl.loop(0, each)
        def _(i):
            z = q * each + i

            @pl.when(z != zi)
            def _():
                remote(chunk(z, xi), chunk(z, xi), s3s.at[z], s3r.at[z], at()).wait_recv()

        @pl.loop(1, x_n)
        def _(i):
            send4(lax.rem(xi + i, x_n), q).start()

    for j in range(1, y_n):
        y = lax.rem(yi + (j if j < 2 else y_n + 1 - j), y_n)
        for c in range(c_n):
            for h in range(zh_n):
                got_g(y * c_n + c, h).wait_recv()
        turn(y)

    @pl.loop(1, x_n)
    def _(i):
        x = lax.rem(xi + i, x_n)
        for q in range(quarters):
            remote(quarter(q, x), quarter(q, x), s4s.at[x, q], s4r.at[x, q], at()).wait_recv()

    @pl.loop(0, zh_n * tiles)
    def _(i):
        h, n = lax.div(i, tiles), lax.rem(i, tiles)
        columns = pl.ds(pl.multiple_of(n * wide_n, wide_n), wide_n)
        damping = 0.1 * jnp.mean(eigs[h], axis=1, keepdims=True)
        product = jnp.dot(chosen[h], rot[h, :, columns], preferred_element_type=F32)
        asked[h, :, columns] = (product / (eigs[h, :, columns] + damping)).astype(BF16)

    def score(y):
        some = pl.ds(pl.multiple_of(y * c_n * rows, c_n * rows), c_n * rows)
        total = None
        for h in range(zh_n):
            term = lax.dot_general(
                turned[h, some, :], asked[h], (((1,), (1,)), ((), ())), preferred_element_type=F32
            )
            total = term if total is None else total + term
        part[pl.ds(y * c_n, c_n)] = total.reshape(c_n, rows, total.shape[1])

    def send_p(t):
        return remote(part.at[t], parts.at[ti], sps.at[t], spr.at[ti], at(t=t))

    @pl.loop(1, y_n)
    def _(j):
        y = lax.rem(yi + j, y_n)
        score(y)
        for c in range(c_n):
            send_p(y * c_n + c).start()

    score(yi)
    send_p(sibling).start()
    parts[ti] = part[ti]

    @pl.loop(1, t_n)
    def _(i):
        t = jnp.bitwise_xor(ti, i)
        remote(parts.at[t], parts.at[t], sps.at[t], spr.at[t], at()).wait_recv()

    total = parts[0]
    for t in range(1, t_n):
        total += parts[t]
    out_ref[...] = total * (1.0 / math.sqrt(modules * width))

    @pl.loop(1, zl_n)
    def _(i):
        send1(lax.rem(zl + i, zl_n)).wait_send()

    @pl.loop(1, z_n)
    def _(i):
        send3(lax.rem(zi + i, z_n)).wait_send()

    @pl.loop(1, x_n)
    def _(i):
        x = lax.rem(xi + i, x_n)
        send2(x).wait_send()
        for q in range(quarters):
            send4(x, q).wait_send()

    @pl.loop(1, t_n)
    def _(i):
        t = jnp.bitwise_xor(ti, i)
        send_p(t).wait_send()
        for h in range(zh_n):
            send_g(t, h).wait_send()


def local(dims, train_grads, query_grads, basis_out, basis_in, eigenvalues, owner_groups, module_order):
    zl_n, x_n, zh_n, y_n, c_n = dims
    rows, modules, width = train_grads.shape
    held, side = query_grads.shape[1], basis_out.shape[1]
    t_n, z_n, piece = y_n * c_n, zh_n * zl_n, width // zl_n
    asks = owner_groups.shape[0] * held
    vmem, smem = pl.BlockSpec(memory_space=pltpu.VMEM), pl.BlockSpec(memory_space=pltpu.SMEM)
    dma = pltpu.SemaphoreType.DMA
    return pl.pallas_call(
        functools.partial(kernel, dims),
        out_shape=jax.ShapeDtypeStruct((rows, asks), F32),
        in_specs=[vmem] * 5 + [smem] * 2,
        out_specs=vmem,
        scratch_shapes=[
            pltpu.VMEM((16 * modules, 16 * modules), BF16),
            pltpu.VMEM((modules, rows, width), BF16),
            pltpu.VMEM((zh_n, t_n * rows, width), BF16),
            pltpu.VMEM((zh_n, width, width), BF16),
            pltpu.VMEM((zh_n, t_n * rows, width), BF16),
            pltpu.VMEM((zh_n, 2, side, 128), BF16),
            pltpu.VMEM((zh_n, 1, width), F32),
            pltpu.VMEM((zl_n, held, piece), BF16),
            pltpu.VMEM((x_n, held, piece), BF16),
            pltpu.VMEM((x_n, held, piece), BF16),
            pltpu.VMEM((zh_n, asks, width), BF16),
            pltpu.VMEM((zh_n, asks, width), BF16),
            pltpu.VMEM((t_n, rows, asks), F32),
            pltpu.VMEM((t_n, rows, asks), F32),
            dma((zl_n,)),
            dma((zl_n,)),
            dma((x_n,)),
            dma((x_n,)),
            dma((z_n,)),
            dma((z_n,)),
            dma((x_n, 4)),
            dma((x_n, 4)),
            dma((t_n, zh_n)),
            dma((t_n, zh_n)),
            dma((2,)),
            dma((2,)),
            dma((t_n,)),
            dma((t_n,)),
        ],
        compiler_params=pltpu.CompilerParams(
            collective_id=0, has_side_effects=True, vmem_limit_bytes=40 << 20
        ),
    )(
        train_grads,
        query_grads.reshape(held, width),
        basis_out[0],
        basis_in[0],
        eigenvalues,
        owner_groups,
        module_order,
    )


def solution(mesh, layout=(X, ZH, Y, C)):
    x_n, zh_n, y_n, c_n = layout
    dims = (mesh.shape["group"] // x_n, x_n, zh_n, y_n, c_n)
    in_specs = (
        P(("group", "module"), None, None),
        P("group", None, "module", None),
        P("module", None, None),
        P("module", None, None),
        P("module", None),
        P(),
        P(),
    )
    out_specs = P(("group", "module"), None)
    return jax.shard_map(
        functools.partial(local, dims), mesh=mesh, in_specs=in_specs, out_specs=out_specs, check_vma=False
    )
```

```python
import functools
import math

import jax
import jax.numpy as jnp
from jax import lax
from jax.experimental import pallas as pl
from jax.experimental.pallas import tpu as pltpu
from jax.sharding import PartitionSpec as P

ZH, Y, C = 2, 4, 2
X = 4
F32, BF16 = jnp.float32, jnp.bfloat16


def kernel(
    dims,
    train_hbm,
    query_hbm,
    bout_hbm,
    bin_hbm,
    eig_hbm,
    owner_hbm,
    order_hbm,
    out_ref,
    train_ref,
    query_ref,
    bout_ref,
    bin_ref,
    owner_ref,
    order_ref,
    fetch_sem,
    perm,
    ordered,
    gathered,
    rot,
    turned,
    bases,
    eigs,
    raw,
    offer,
    offered,
    chosen,
    asked,
    part,
    parts,
    s1s,
    s1r,
    s2s,
    s2r,
    s3s,
    s3r,
    s4s,
    s4r,
    sgs,
    sgr,
    sbs,
    sbr,
    sps,
    spr,
):
    zl_n, x_n, zh_n, y_n, c_n = dims
    t_n = y_n * c_n
    z_n = zh_n * zl_n
    rows, modules, width = train_ref.shape
    held = query_ref.shape[0]
    piece = width // zl_n
    group, module = lax.axis_index("group"), lax.axis_index("module")
    zl, xi = lax.div(group, x_n), lax.rem(group, x_n)
    zh, ti = lax.div(module, t_n), lax.rem(module, t_n)
    yi = lax.div(ti, c_n)
    zi = zh * zl_n + zl

    def at(z=None, x=None, t=None):
        z = zi if z is None else z
        x = xi if x is None else x
        t = ti if t is None else t
        return (lax.rem(z, zl_n) * x_n + x, lax.div(z, zl_n) * t_n + t)

    def remote(src, dst, send, recv, where):
        return pltpu.make_async_remote_copy(
            src_ref=src,
            dst_ref=dst,
            send_sem=send,
            recv_sem=recv,
            device_id=where,
            device_id_type=pl.DeviceIdType.MESH,
        )

    fetches = [
        pltpu.make_async_copy(src, dst, fetch_sem.at[i])
        for i, (src, dst) in enumerate(
            (
                (order_hbm, order_ref),
                (train_hbm, train_ref),
                (query_hbm, query_ref),
                (bout_hbm, bout_ref),
                (bin_hbm, bin_ref),
                (eig_hbm, eigs.at[zh]),
                (owner_hbm, owner_ref),
            )
        )
    ]
    for fetch in fetches:
        fetch.start()

    barrier = pltpu.get_barrier_semaphore()

    def greet(where):
        pl.semaphore_signal(
            barrier, inc=1, device_id=where, device_id_type=pl.DeviceIdType.MESH
        )

    @pl.loop(1, z_n)
    def _(i):
        greet(at(z=lax.rem(zi + i, z_n)))

    @pl.loop(1, x_n)
    def _(i):
        greet(at(x=lax.rem(xi + i, x_n)))

    @pl.loop(1, t_n)
    def _(i):
        greet(at(t=lax.rem(ti + i, t_n)))

    for fetch in fetches:
        fetch.wait()
    batch = 16
    span = batch * modules
    for s in range(modules):
        lane = lax.broadcasted_iota(jnp.int32, (batch, span), 1)
        row = lax.broadcasted_iota(jnp.int32, (batch, span), 0)
        hit = lane == row * modules + order_ref[s]
        perm[pl.ds(s * batch, batch), :] = jnp.where(hit, 1.0, 0.0).astype(BF16)
    for b in range(rows // batch):
        block = train_ref[pl.ds(b * batch, batch)].reshape(span, width)
        moved = jnp.dot(perm[...], block, preferred_element_type=F32).astype(BF16)
        ordered[:, pl.ds(b * batch, batch), :] = moved.reshape(modules, batch, width)

    bases[zh] = jnp.zeros(bases.shape[1:], BF16)
    bases[zh, 0, :, : bout_ref.shape[1]] = bout_ref[...]
    bases[zh, 1, :, : bin_ref.shape[1]] = bin_ref[...]

    pl.semaphore_wait(barrier, z_n + x_n + t_n - 3)

    def send1(z):
        return remote(
            query_ref.at[:, pl.ds(pl.multiple_of(z * piece, piece), piece)],
            raw.at[zl],
            s1s.at[z],
            s1r.at[zl],
            at(z=zh * zl_n + z),
        )

    @pl.loop(1, zl_n)
    def _(i):
        send1(lax.rem(zl + i, zl_n)).start()

    other = zh_n - 1 - zh
    twins = [
        remote(bases.at[zh], bases.at[zh], sbs.at[0], sbr.at[0], at(z=other * zl_n + zl)),
        remote(eigs.at[zh], eigs.at[zh], sbs.at[1], sbr.at[1], at(z=other * zl_n + zl)),
    ]
    for twin in twins:
        twin.start()

    def send_g(t, h):
        return remote(
            ordered.at[h * t_n + t],
            gathered.at[h, pl.ds(pl.multiple_of(ti * rows, rows), rows)],
            sgs.at[t, h],
            sgr.at[ti, h],
            at(t=t),
        )

    def got_g(t, h):
        return remote(
            ordered.at[h * t_n + t],
            gathered.at[h, pl.ds(pl.multiple_of(t * rows, rows), rows)],
            sgs.at[t, h],
            sgr.at[t, h],
            at(t=t),
        )

    near = [j for j in range(1, y_n) if j != 2]
    far = [j for j in range(1, y_n) if j == 2]
    for j in [0] + near + far:
        for c in range(1 if j == 0 else 0, c_n):
            for h in range(zh_n):
                send_g(jnp.bitwise_xor(ti, j * c_n + c), h).start()

    for h in range(zh_n):
        gathered[h, pl.ds(pl.multiple_of(ti * rows, rows), rows)] = ordered[h * t_n + ti]

    def build(h):
        side = bout_ref.shape[1]
        lane = lax.broadcasted_iota(jnp.int32, (bases.shape[3], width), 1)
        row = lax.broadcasted_iota(jnp.int32, (bases.shape[3], width), 0)
        wide = jnp.where(lax.div(lane, side) == row, 1.0, 0.0).astype(BF16)
        tiled = jnp.where(lax.rem(lane, side) == row, 1.0, 0.0).astype(BF16)
        outer = jnp.dot(bases[h, 0], wide, preferred_element_type=F32)
        inner = jnp.dot(bases[h, 1], tiled, preferred_element_type=F32)
        for a in range(side):
            rot[h, pl.ds(a * side, side), :] = (outer[a : a + 1] * inner).astype(BF16)

    build(zh)

    raw[zl] = query_ref[:, pl.ds(pl.multiple_of(zl * piece, piece), piece)]

    @pl.loop(1, zl_n)
    def _(i):
        z = lax.rem(zl + i, zl_n)
        remote(raw.at[z], raw.at[z], s1s.at[z], s1r.at[z], at()).wait_recv()

    for k in range(x_n):
        offer[k] = raw[lax.div(owner_ref[k], x_n)]

    def send2(x):
        return remote(offer.at[x], offered.at[xi], s2s.at[x], s2r.at[xi], at(x=x))

    @pl.loop(1, x_n)
    def _(i):
        send2(lax.rem(xi + i, x_n)).start()

    offered[xi] = offer[xi]

    @pl.loop(1, x_n)
    def _(i):
        x = lax.rem(xi + i, x_n)
        remote(offer.at[x], offered.at[x], s2s.at[x], s2r.at[x], at()).wait_recv()

    lines = pl.ds(pl.multiple_of(xi * held, held), held)
    chosen[zh, lines, pl.ds(pl.multiple_of(zl * piece, piece), piece)] = offered[
        lax.rem(owner_ref[xi], x_n)
    ]

    def chunk(z, k):
        return chosen.at[
            lax.div(z, zl_n),
            pl.ds(pl.multiple_of(k * held, held), held),
            pl.ds(pl.multiple_of(lax.rem(z, zl_n) * piece, piece), piece),
        ]

    def send3(z):
        return remote(chunk(zi, xi), chunk(zi, xi), s3s.at[z], s3r.at[zi], at(z=z))

    @pl.loop(1, z_n)
    def _(i):
        send3(lax.rem(zi + i, z_n)).start()

    for twin in twins:
        twin.wait_send()
    for i, buf in enumerate((bases, eigs)):
        remote(buf.at[other], buf.at[other], sbs.at[i], sbr.at[i], at()).wait_recv()
    build(other)

    wide_n = 256
    tiles = width // wide_n

    def turn(y):
        @pl.loop(0, zh_n * tiles)
        def _(i):
            h, n = lax.div(i, tiles), lax.rem(i, tiles)
            some = pl.ds(pl.multiple_of(y * c_n * rows, c_n * rows), c_n * rows)
            columns = pl.ds(pl.multiple_of(n * wide_n, wide_n), wide_n)
            turned[h, some, columns] = jnp.dot(
                gathered[h, some, :], rot[h, :, columns], preferred_element_type=F32
            ).astype(BF16)

    sibling = jnp.bitwise_xor(ti, 1)
    for h in range(zh_n):
        got_g(sibling, h).wait_recv()
    turn(yi)

    quarters = s4s.shape[1]
    each = z_n // quarters

    def quarter(q, k):
        per = quarters // zh_n
        return chosen.at[
            lax.div(q, per),
            pl.ds(pl.multiple_of(k * held, held), held),
            pl.ds(pl.multiple_of(lax.rem(q, per) * each * piece, each * piece), each * piece),
        ]

    def send4(x, q):
        return remote(quarter(q, xi), quarter(q, xi), s4s.at[x, q], s4r.at[xi, q], at(x=x))

    home = lax.div(zi, each)
    for j in (0, 1, quarters - 1, 2):
        q = lax.rem(home + j, quarters)

        @pl.loop(0, each)
        def _(i):
            z = q * each + i

            @pl.when(z != zi)
            def _():
                remote(chunk(z, xi), chunk(z, xi), s3s.at[z], s3r.at[z], at()).wait_recv()

        @pl.loop(1, x_n)
        def _(i):
            send4(lax.rem(xi + i, x_n), q).start()

    def await_g(y):
        for c in range(c_n):
            for h in range(zh_n):
                got_g(y * c_n + c, h).wait_recv()

    for j in near:
        await_g(jnp.bitwise_xor(yi, j))
        turn(jnp.bitwise_xor(yi, j))

    @pl.loop(1, x_n)
    def _(i):
        x = lax.rem(xi + i, x_n)
        for q in range(quarters):
            remote(quarter(q, x), quarter(q, x), s4s.at[x, q], s4r.at[x, q], at()).wait_recv()

    @pl.loop(0, zh_n * tiles)
    def _(i):
        h, n = lax.div(i, tiles), lax.rem(i, tiles)
        columns = pl.ds(pl.multiple_of(n * wide_n, wide_n), wide_n)
        damping = 0.1 * jnp.mean(eigs[h], axis=1, keepdims=True)
        product = jnp.dot(chosen[h], rot[h, :, columns], preferred_element_type=F32)
        asked[h, :, columns] = (product / (eigs[h, :, columns] + damping)).astype(BF16)

    def score(y):
        some = pl.ds(pl.multiple_of(y * c_n * rows, c_n * rows), c_n * rows)
        total = None
        for h in range(zh_n):
            term = lax.dot_general(
                turned[h, some, :], asked[h], (((1,), (1,)), ((), ())), preferred_element_type=F32
            )
            total = term if total is None else total + term
        part[pl.ds(y * c_n, c_n)] = total.reshape(c_n, rows, total.shape[1])

    def send_p(t):
        return remote(part.at[t], parts.at[ti], sps.at[t], spr.at[ti], at(t=t))

    for j in near + [0] + far:
        y = jnp.bitwise_xor(yi, j)
        if j in far:
            await_g(y)
            turn(y)
        score(y)
        for c in range(c_n):
            if j:
                send_p(y * c_n + c).start()
        if j == 0:
            send_p(sibling).start()
            parts[ti] = part[ti]

    @pl.loop(1, t_n)
    def _(i):
        t = jnp.bitwise_xor(ti, i)
        remote(parts.at[t], parts.at[t], sps.at[t], spr.at[t], at()).wait_recv()

    total = parts[0]
    for t in range(1, t_n):
        total += parts[t]
    out_ref[...] = total * (1.0 / math.sqrt(modules * width))

    @pl.loop(1, zl_n)
    def _(i):
        send1(lax.rem(zl + i, zl_n)).wait_send()

    @pl.loop(1, z_n)
    def _(i):
        send3(lax.rem(zi + i, z_n)).wait_send()

    @pl.loop(1, x_n)
    def _(i):
        x = lax.rem(xi + i, x_n)
        send2(x).wait_send()
        for q in range(quarters):
            send4(x, q).wait_send()

    @pl.loop(1, t_n)
    def _(i):
        t = jnp.bitwise_xor(ti, i)
        send_p(t).wait_send()
        for h in range(zh_n):
            send_g(t, h).wait_send()


def local(dims, train_grads, query_grads, basis_out, basis_in, eigenvalues, owner_groups, module_order):
    zl_n, x_n, zh_n, y_n, c_n = dims
    rows, modules, width = train_grads.shape
    held, side = query_grads.shape[1], basis_out.shape[1]
    t_n, z_n, piece = y_n * c_n, zh_n * zl_n, width // zl_n
    asks = owner_groups.shape[0] * held
    dma = pltpu.SemaphoreType.DMA
    return pl.pallas_call(
        functools.partial(kernel, dims),
        out_shape=jax.ShapeDtypeStruct((rows, asks), F32),
        in_specs=[pl.BlockSpec(memory_space=pl.ANY)] * 7,
        out_specs=pl.BlockSpec(memory_space=pltpu.VMEM),
        scratch_shapes=[
            pltpu.VMEM((rows, modules, width), BF16),
            pltpu.VMEM((held, width), BF16),
            pltpu.VMEM((side, side), BF16),
            pltpu.VMEM((side, side), BF16),
            pltpu.SMEM(owner_groups.shape, jnp.int32),
            pltpu.SMEM(module_order.shape, jnp.int32),
            dma((7,)),
            pltpu.VMEM((16 * modules, 16 * modules), BF16),
            pltpu.VMEM((modules, rows, width), BF16),
            pltpu.VMEM((zh_n, t_n * rows, width), BF16),
            pltpu.VMEM((zh_n, width, width), BF16),
            pltpu.VMEM((zh_n, t_n * rows, width), BF16),
            pltpu.VMEM((zh_n, 2, side, 128), BF16),
            pltpu.VMEM((zh_n, 1, width), F32),
            pltpu.VMEM((zl_n, held, piece), BF16),
            pltpu.VMEM((x_n, held, piece), BF16),
            pltpu.VMEM((x_n, held, piece), BF16),
            pltpu.VMEM((zh_n, asks, width), BF16),
            pltpu.VMEM((zh_n, asks, width), BF16),
            pltpu.VMEM((t_n, rows, asks), F32),
            pltpu.VMEM((t_n, rows, asks), F32),
            dma((zl_n,)),
            dma((zl_n,)),
            dma((x_n,)),
            dma((x_n,)),
            dma((z_n,)),
            dma((z_n,)),
            dma((x_n, 4)),
            dma((x_n, 4)),
            dma((t_n, zh_n)),
            dma((t_n, zh_n)),
            dma((2,)),
            dma((2,)),
            dma((t_n,)),
            dma((t_n,)),
        ],
        compiler_params=pltpu.CompilerParams(
            collective_id=0, has_side_effects=True, vmem_limit_bytes=60 << 20
        ),
    )(
        train_grads,
        query_grads.reshape(held, width),
        basis_out[0],
        basis_in[0],
        eigenvalues,
        owner_groups,
        module_order,
    )


def solution(mesh, layout=(X, ZH, Y, C)):
    x_n, zh_n, y_n, c_n = layout
    dims = (mesh.shape["group"] // x_n, x_n, zh_n, y_n, c_n)
    in_specs = (
        P(("group", "module"), None, None),
        P("group", None, "module", None),
        P("module", None, None),
        P("module", None, None),
        P("module", None),
        P(),
        P(),
    )
    out_specs = P(("group", "module"), None)
    return jax.shard_map(
        functools.partial(local, dims), mesh=mesh, in_specs=in_specs, out_specs=out_specs, check_vma=False
    )
```

```python
import functools
import math

import jax
import jax.numpy as jnp
from jax import lax
from jax.experimental import pallas as pl
from jax.experimental.pallas import tpu as pltpu
from jax.sharding import PartitionSpec as P

ZH, Y, C = 2, 4, 2
X = 4
F32, BF16 = jnp.float32, jnp.bfloat16


def kernel(
    dims,
    train_hbm,
    query_hbm,
    bout_hbm,
    bin_hbm,
    eig_hbm,
    owner_hbm,
    order_hbm,
    out_ref,
    train_ref,
    query_ref,
    bout_ref,
    bin_ref,
    owner_ref,
    order_ref,
    fetch_sem,
    perm,
    ordered,
    gathered,
    rot,
    turned,
    bases,
    eigs,
    heard,
    crossed,
    offer,
    offered,
    chosen,
    asked,
    part,
    parts,
    whole,
    s1s,
    s1r,
    s2s,
    s2r,
    s3s,
    s3r,
    s4s,
    s4r,
    sgs,
    sgr,
    sbs,
    sbr,
    sps,
    spr,
):
    zl_n, x_n, zh_n, y_n, c_n = dims
    t_n = y_n * c_n
    z_n = zh_n * zl_n
    rows, modules, width = train_ref.shape
    held = query_ref.shape[0]
    piece = width // zl_n
    group, module = lax.axis_index("group"), lax.axis_index("module")
    zl, xi = lax.div(group, x_n), lax.rem(group, x_n)
    zh, ti = lax.div(module, t_n), lax.rem(module, t_n)
    yi = lax.div(ti, c_n)
    zi = zh * zl_n + zl

    def at(z=None, x=None, t=None):
        z = zi if z is None else z
        x = xi if x is None else x
        t = ti if t is None else t
        return (lax.rem(z, zl_n) * x_n + x, lax.div(z, zl_n) * t_n + t)

    def remote(src, dst, send, recv, where):
        return pltpu.make_async_remote_copy(
            src_ref=src,
            dst_ref=dst,
            send_sem=send,
            recv_sem=recv,
            device_id=where,
            device_id_type=pl.DeviceIdType.MESH,
        )

    fetches = [
        pltpu.make_async_copy(src, dst, fetch_sem.at[i])
        for i, (src, dst) in enumerate(
            (
                (order_hbm, order_ref),
                (train_hbm, train_ref),
                (query_hbm, query_ref),
                (bout_hbm, bout_ref),
                (bin_hbm, bin_ref),
                (eig_hbm, eigs.at[zh]),
                (owner_hbm, owner_ref),
            )
        )
    ]
    for fetch in fetches:
        fetch.start()

    barrier = pltpu.get_barrier_semaphore()

    def greet(where):
        pl.semaphore_signal(
            barrier, inc=1, device_id=where, device_id_type=pl.DeviceIdType.MESH
        )

    greet(at(z=lax.rem(zi + 1, z_n)))
    greet(at(z=lax.rem(zi + z_n - 1, z_n)))

    @pl.loop(1, x_n)
    def _(i):
        greet(at(x=lax.rem(xi + i, x_n)))

    @pl.loop(1, t_n)
    def _(i):
        greet(at(t=lax.rem(ti + i, t_n)))

    order_in, train_in, query_in, *small_in = fetches
    query_in.wait()
    pl.semaphore_wait(barrier, x_n + t_n)

    def send1(x):
        return remote(query_ref, crossed.at[xi], s1s.at[x], s1r.at[xi], at(x=x))

    @pl.loop(1, x_n)
    def _(i):
        send1(lax.rem(xi + i, x_n)).start()

    def tell(step):
        d = 1 << step
        for z in (lax.rem(zi + d, z_n), lax.rem(zi + z_n - d, z_n)):
            pl.semaphore_signal(
                heard.at[step], inc=1, device_id=at(z=z), device_id_type=pl.DeviceIdType.MESH
            )

    def hear(step):
        pl.semaphore_wait(heard.at[step], 2)
        if step + 1 < steps:
            tell(step + 1)

    steps = (z_n // 2).bit_length() - 1
    tell(0)

    batch = 16
    span = batch * modules
    order_in.wait()
    for s in range(modules):
        lane = lax.broadcasted_iota(jnp.int32, (batch, span), 1)
        row = lax.broadcasted_iota(jnp.int32, (batch, span), 0)
        hit = lane == row * modules + order_ref[s]
        perm[pl.ds(s * batch, batch), :] = jnp.where(hit, 1.0, 0.0).astype(BF16)
    train_in.wait()
    for b in range(rows // batch):
        block = train_ref[pl.ds(b * batch, batch)].reshape(span, width)
        moved = jnp.dot(perm[...], block, preferred_element_type=F32).astype(BF16)
        ordered[:, pl.ds(b * batch, batch), :] = moved.reshape(modules, batch, width)
    hear(0)

    def send_g(t, h):
        return remote(
            ordered.at[h * t_n + t],
            gathered.at[h, pl.ds(pl.multiple_of(ti * rows, rows), rows)],
            sgs.at[t, h],
            sgr.at[ti, h],
            at(t=t),
        )

    def got_g(t, h):
        return remote(
            ordered.at[h * t_n + t],
            gathered.at[h, pl.ds(pl.multiple_of(t * rows, rows), rows)],
            sgs.at[t, h],
            sgr.at[t, h],
            at(t=t),
        )

    near = [j for j in range(1, y_n) if j != 2]
    far = [j for j in range(1, y_n) if j == 2]
    for j in [0] + near + far:
        for c in range(1 if j == 0 else 0, c_n):
            for h in range(zh_n):
                send_g(jnp.bitwise_xor(ti, j * c_n + c), h).start()

    for fetch in small_in:
        fetch.wait()

    bases[zh] = jnp.zeros(bases.shape[1:], BF16)
    bases[zh, 0, :, : bout_ref.shape[1]] = bout_ref[...]
    bases[zh, 1, :, : bin_ref.shape[1]] = bin_ref[...]

    if steps > 1:
        hear(1)

    def build(h):
        side = bout_ref.shape[1]
        lane = lax.broadcasted_iota(jnp.int32, (bases.shape[3], width), 1)
        row = lax.broadcasted_iota(jnp.int32, (bases.shape[3], width), 0)
        wide = jnp.where(lax.div(lane, side) == row, 1.0, 0.0).astype(BF16)
        tiled = jnp.where(lax.rem(lane, side) == row, 1.0, 0.0).astype(BF16)
        outer = jnp.dot(bases[h, 0], wide, preferred_element_type=F32)
        inner = jnp.dot(bases[h, 1], tiled, preferred_element_type=F32)
        for a in range(side):
            rot[h, pl.ds(a * side, side), :] = (outer[a : a + 1] * inner).astype(BF16)

    build(zh)

    for h in range(zh_n):
        gathered[h, pl.ds(pl.multiple_of(ti * rows, rows), rows)] = ordered[h * t_n + ti]

    crossed[xi] = query_ref[...]

    @pl.loop(1, x_n)
    def _(i):
        x = lax.rem(xi + i, x_n)
        remote(query_ref, crossed.at[x], s1s.at[x], s1r.at[x], at()).wait_recv()

    offer[...] = crossed[lax.rem(owner_ref[xi], x_n)]
    for step in range(min(2, steps), steps):
        hear(step)

    def span_of(z):
        return pl.ds(pl.multiple_of(z * piece, piece), piece)

    def send2(z):
        return remote(
            offer.at[:, span_of(z)], offered.at[zl], s2s.at[z], s2r.at[zl], at(z=zh * zl_n + z)
        )

    @pl.loop(1, zl_n)
    def _(i):
        send2(lax.rem(zl + i, zl_n)).start()

    other = zh_n - 1 - zh
    twins = [
        remote(bases.at[zh], bases.at[zh], sbs.at[0], sbr.at[0], at(z=other * zl_n + zl)),
        remote(eigs.at[zh], eigs.at[zh], sbs.at[1], sbr.at[1], at(z=other * zl_n + zl)),
    ]
    for twin in twins:
        twin.start()

    offered[zl] = offer[:, span_of(zl)]

    @pl.loop(1, zl_n)
    def _(i):
        z = lax.rem(zl + i, zl_n)
        remote(offered.at[z], offered.at[z], s2s.at[z], s2r.at[z], at()).wait_recv()

    lines = pl.ds(pl.multiple_of(xi * held, held), held)
    chosen[zh, lines, span_of(zl)] = offered[lax.div(owner_ref[xi], x_n)]

    def chunk(z, k):
        return chosen.at[
            lax.div(z, zl_n),
            pl.ds(pl.multiple_of(k * held, held), held),
            pl.ds(pl.multiple_of(lax.rem(z, zl_n) * piece, piece), piece),
        ]

    def send3(z):
        return remote(chunk(zi, xi), chunk(zi, xi), s3s.at[z], s3r.at[zi], at(z=z))

    @pl.loop(1, z_n)
    def _(i):
        send3(lax.rem(zi + i, z_n)).start()

    for twin in twins:
        twin.wait_send()
    for i, buf in enumerate((bases, eigs)):
        remote(buf.at[other], buf.at[other], sbs.at[i], sbr.at[i], at()).wait_recv()
    build(other)

    wide_n = 256
    tiles = width // wide_n

    def turn(y):
        @pl.loop(0, zh_n * tiles)
        def _(i):
            h, n = lax.div(i, tiles), lax.rem(i, tiles)
            some = pl.ds(pl.multiple_of(y * c_n * rows, c_n * rows), c_n * rows)
            columns = pl.ds(pl.multiple_of(n * wide_n, wide_n), wide_n)
            turned[h, some, columns] = jnp.dot(
                gathered[h, some, :], rot[h, :, columns], preferred_element_type=F32
            ).astype(BF16)

    sibling = jnp.bitwise_xor(ti, 1)
    for h in range(zh_n):
        got_g(sibling, h).wait_recv()
    turn(yi)

    quarters = s4s.shape[1]
    each = z_n // quarters

    def quarter(q, k):
        per = quarters // zh_n
        return chosen.at[
            lax.div(q, per),
            pl.ds(pl.multiple_of(k * held, held), held),
            pl.ds(pl.multiple_of(lax.rem(q, per) * each * piece, each * piece), each * piece),
        ]

    def send4(x, q):
        return remote(quarter(q, xi), quarter(q, xi), s4s.at[x, q], s4r.at[xi, q], at(x=x))

    home = lax.div(zi, each)
    for j in (0, 1, quarters - 1, 2):
        q = lax.rem(home + j, quarters)

        @pl.loop(0, each)
        def _(i):
            z = q * each + i

            @pl.when(z != zi)
            def _():
                remote(chunk(z, xi), chunk(z, xi), s3s.at[z], s3r.at[z], at()).wait_recv()

        @pl.loop(1, x_n)
        def _(i):
            send4(lax.rem(xi + i, x_n), q).start()

    def await_g(y):
        for c in range(c_n):
            for h in range(zh_n):
                got_g(y * c_n + c, h).wait_recv()

    for j in near:
        await_g(jnp.bitwise_xor(yi, j))
        turn(jnp.bitwise_xor(yi, j))

    @pl.loop(1, x_n)
    def _(i):
        x = lax.rem(xi + i, x_n)
        for q in range(quarters):
            remote(quarter(q, x), quarter(q, x), s4s.at[x, q], s4r.at[x, q], at()).wait_recv()

    @pl.loop(0, zh_n * tiles)
    def _(i):
        h, n = lax.div(i, tiles), lax.rem(i, tiles)
        columns = pl.ds(pl.multiple_of(n * wide_n, wide_n), wide_n)
        damping = 0.1 * jnp.mean(eigs[h], axis=1, keepdims=True)
        product = jnp.dot(chosen[h], rot[h, :, columns], preferred_element_type=F32)
        asked[h, :, columns] = (product / (eigs[h, :, columns] + damping)).astype(BF16)

    def score(y):
        some = pl.ds(pl.multiple_of(y * c_n * rows, c_n * rows), c_n * rows)
        total = None
        for h in range(zh_n):
            term = lax.dot_general(
                turned[h, some, :], asked[h], (((1,), (1,)), ((), ())), preferred_element_type=F32
            )
            total = term if total is None else total + term
        part[pl.ds(y * c_n, c_n)] = total.reshape(c_n, rows, total.shape[1]).astype(BF16)
        return total

    def send_p(t):
        return remote(part.at[t], parts.at[ti], sps.at[t], spr.at[ti], at(t=t))

    for j in near + [0] + far:
        y = jnp.bitwise_xor(yi, j)
        if j in far:
            await_g(y)
            turn(y)
        total = score(y)
        for c in range(c_n):
            if j:
                send_p(y * c_n + c).start()
        if j == 0:
            send_p(sibling).start()
            whole[...] = total.reshape(c_n, rows, total.shape[1])

    @pl.loop(1, t_n)
    def _(i):
        t = jnp.bitwise_xor(ti, i)
        remote(parts.at[t], parts.at[t], sps.at[t], spr.at[t], at()).wait_recv()

    total = whole[lax.rem(ti, c_n)]
    for i in range(1, t_n):
        total += parts[jnp.bitwise_xor(ti, i)].astype(F32)
    out_ref[...] = total * (1.0 / math.sqrt(modules * width))

    @pl.loop(1, zl_n)
    def _(i):
        send2(lax.rem(zl + i, zl_n)).wait_send()

    @pl.loop(1, z_n)
    def _(i):
        send3(lax.rem(zi + i, z_n)).wait_send()

    @pl.loop(1, x_n)
    def _(i):
        x = lax.rem(xi + i, x_n)
        send1(x).wait_send()
        for q in range(quarters):
            send4(x, q).wait_send()

    @pl.loop(1, t_n)
    def _(i):
        t = jnp.bitwise_xor(ti, i)
        send_p(t).wait_send()
        for h in range(zh_n):
            send_g(t, h).wait_send()


def local(dims, train_grads, query_grads, basis_out, basis_in, eigenvalues, owner_groups, module_order):
    zl_n, x_n, zh_n, y_n, c_n = dims
    rows, modules, width = train_grads.shape
    held, side = query_grads.shape[1], basis_out.shape[1]
    t_n, z_n, piece = y_n * c_n, zh_n * zl_n, width // zl_n
    asks = owner_groups.shape[0] * held
    dma = pltpu.SemaphoreType.DMA
    return pl.pallas_call(
        functools.partial(kernel, dims),
        out_shape=jax.ShapeDtypeStruct((rows, asks), F32),
        in_specs=[pl.BlockSpec(memory_space=pl.ANY)] * 7,
        out_specs=pl.BlockSpec(memory_space=pltpu.VMEM),
        scratch_shapes=[
            pltpu.VMEM((rows, modules, width), BF16),
            pltpu.VMEM((held, width), BF16),
            pltpu.VMEM((side, side), BF16),
            pltpu.VMEM((side, side), BF16),
            pltpu.SMEM(owner_groups.shape, jnp.int32),
            pltpu.SMEM(module_order.shape, jnp.int32),
            dma((7,)),
            pltpu.VMEM((16 * modules, 16 * modules), BF16),
            pltpu.VMEM((modules, rows, width), BF16),
            pltpu.VMEM((zh_n, t_n * rows, width), BF16),
            pltpu.VMEM((zh_n, width, width), BF16),
            pltpu.VMEM((zh_n, t_n * rows, width), BF16),
            pltpu.VMEM((zh_n, 2, side, 128), BF16),
            pltpu.VMEM((zh_n, 1, width), F32),
            pltpu.SemaphoreType.REGULAR(((z_n // 2).bit_length() - 1,)),
            pltpu.VMEM((x_n, held, width), BF16),
            pltpu.VMEM((held, width), BF16),
            pltpu.VMEM((zl_n, held, piece), BF16),
            pltpu.VMEM((zh_n, asks, width), BF16),
            pltpu.VMEM((zh_n, asks, width), BF16),
            pltpu.VMEM((t_n, rows, asks), BF16),
            pltpu.VMEM((t_n, rows, asks), BF16),
            pltpu.VMEM((c_n, rows, asks), F32),
            dma((x_n,)),
            dma((x_n,)),
            dma((zl_n,)),
            dma((zl_n,)),
            dma((z_n,)),
            dma((z_n,)),
            dma((x_n, 4)),
            dma((x_n, 4)),
            dma((t_n, zh_n)),
            dma((t_n, zh_n)),
            dma((2,)),
            dma((2,)),
            dma((t_n,)),
            dma((t_n,)),
        ],
        compiler_params=pltpu.CompilerParams(
            collective_id=0, has_side_effects=True, vmem_limit_bytes=60 << 20
        ),
    )(
        train_grads,
        query_grads.reshape(held, width),
        basis_out[0],
        basis_in[0],
        eigenvalues,
        owner_groups,
        module_order,
    )


def solution(mesh, layout=(X, ZH, Y, C)):
    x_n, zh_n, y_n, c_n = layout
    dims = (mesh.shape["group"] // x_n, x_n, zh_n, y_n, c_n)
    in_specs = (
        P(("group", "module"), None, None),
        P("group", None, "module", None),
        P("module", None, None),
        P("module", None, None),
        P("module", None),
        P(),
        P(),
    )
    out_specs = P(("group", "module"), None)
    return jax.shard_map(
        functools.partial(local, dims), mesh=mesh, in_specs=in_specs, out_specs=out_specs, check_vma=False
    )
```

```python
import functools
import math

import jax
import jax.numpy as jnp
from jax import lax
from jax.experimental import pallas as pl
from jax.experimental.pallas import tpu as pltpu
from jax.sharding import PartitionSpec as P

ZH, Y, C = 2, 4, 2
X = 4
F32, BF16 = jnp.float32, jnp.bfloat16


def kernel(
    dims,
    train_hbm,
    query_hbm,
    bout_hbm,
    bin_hbm,
    eig_hbm,
    owner_hbm,
    order_hbm,
    out_ref,
    train_ref,
    query_ref,
    bout_ref,
    bin_ref,
    owner_ref,
    order_ref,
    fetch_sem,
    perm,
    ordered,
    gathered,
    rot,
    turned,
    bases,
    eigs,
    heard,
    crossed,
    offer,
    offered,
    chosen,
    asked,
    total_asked,
    part,
    parts,
    whole,
    s1s,
    s1r,
    s2s,
    s2r,
    s3s,
    s3r,
    s4s,
    s4r,
    sgs,
    sgr,
    sbs,
    sbr,
    sps,
    spr,
):
    zl_n, x_n, zh_n, y_n, c_n = dims
    t_n = y_n * c_n
    z_n = zh_n * zl_n
    rows, modules, width = train_ref.shape
    held = query_ref.shape[0]
    piece = width // zl_n
    group, module = lax.axis_index("group"), lax.axis_index("module")
    zl, xi = lax.div(group, x_n), lax.rem(group, x_n)
    zh, ti = lax.div(module, t_n), lax.rem(module, t_n)
    yi = lax.div(ti, c_n)
    zi = zh * zl_n + zl

    def at(z=None, x=None, t=None):
        z = zi if z is None else z
        x = xi if x is None else x
        t = ti if t is None else t
        return (lax.rem(z, zl_n) * x_n + x, lax.div(z, zl_n) * t_n + t)

    def remote(src, dst, send, recv, where):
        return pltpu.make_async_remote_copy(
            src_ref=src,
            dst_ref=dst,
            send_sem=send,
            recv_sem=recv,
            device_id=where,
            device_id_type=pl.DeviceIdType.MESH,
        )

    fetches = [
        pltpu.make_async_copy(src, dst, fetch_sem.at[i])
        for i, (src, dst) in enumerate(
            (
                (order_hbm, order_ref),
                (train_hbm, train_ref),
                (query_hbm, query_ref),
                (bout_hbm, bout_ref),
                (bin_hbm, bin_ref),
                (eig_hbm, eigs.at[zh]),
                (owner_hbm, owner_ref),
            )
        )
    ]
    for fetch in fetches:
        fetch.start()

    barrier = pltpu.get_barrier_semaphore()

    def greet(where):
        pl.semaphore_signal(
            barrier, inc=1, device_id=where, device_id_type=pl.DeviceIdType.MESH
        )

    greet(at(z=lax.rem(zi + 1, z_n)))
    greet(at(z=lax.rem(zi + z_n - 1, z_n)))

    @pl.loop(1, x_n)
    def _(i):
        greet(at(x=lax.rem(xi + i, x_n)))

    @pl.loop(1, t_n)
    def _(i):
        greet(at(t=lax.rem(ti + i, t_n)))

    order_in, train_in, query_in, *small_in = fetches
    query_in.wait()
    pl.semaphore_wait(barrier, x_n + t_n)

    def send1(x):
        return remote(query_ref, crossed.at[xi], s1s.at[x], s1r.at[xi], at(x=x))

    @pl.loop(1, x_n)
    def _(i):
        send1(lax.rem(xi + i, x_n)).start()

    def tell(step):
        d = 1 << step
        for z in (lax.rem(zi + d, z_n), lax.rem(zi + z_n - d, z_n)):
            pl.semaphore_signal(
                heard.at[step], inc=1, device_id=at(z=z), device_id_type=pl.DeviceIdType.MESH
            )

    def hear(step):
        pl.semaphore_wait(heard.at[step], 2)
        if step + 1 < steps:
            tell(step + 1)

    steps = (z_n // 2).bit_length() - 1
    tell(0)

    batch = 16
    span = batch * modules
    order_in.wait()
    for s in range(modules):
        lane = lax.broadcasted_iota(jnp.int32, (batch, span), 1)
        row = lax.broadcasted_iota(jnp.int32, (batch, span), 0)
        hit = lane == row * modules + order_ref[s]
        perm[pl.ds(s * batch, batch), :] = jnp.where(hit, 1.0, 0.0).astype(BF16)
    train_in.wait()
    for b in range(rows // batch):
        block = train_ref[pl.ds(b * batch, batch)].reshape(span, width)
        moved = jnp.dot(perm[...], block, preferred_element_type=F32).astype(BF16)
        ordered[:, pl.ds(b * batch, batch), :] = moved.reshape(modules, batch, width)
    hear(0)

    def send_g(t, h):
        return remote(
            ordered.at[h * t_n + t],
            gathered.at[h, pl.ds(pl.multiple_of(ti * rows, rows), rows)],
            sgs.at[t, h],
            sgr.at[ti, h],
            at(t=t),
        )

    def got_g(t, h):
        return remote(
            ordered.at[h * t_n + t],
            gathered.at[h, pl.ds(pl.multiple_of(t * rows, rows), rows)],
            sgs.at[t, h],
            sgr.at[t, h],
            at(t=t),
        )

    near = [j for j in range(1, y_n) if j != 2]
    far = [j for j in range(1, y_n) if j == 2]
    for j in [0] + near + far:
        for c in range(1 if j == 0 else 0, c_n):
            for h in range(zh_n):
                send_g(jnp.bitwise_xor(ti, j * c_n + c), h).start()

    for fetch in small_in:
        fetch.wait()

    bases[zh] = jnp.zeros(bases.shape[1:], BF16)
    side = bout_ref.shape[1]
    bases[zh, :, :side] = bout_ref[...]
    bases[zh, :, side : 2 * side] = bin_ref[...]

    if steps > 1:
        hear(1)

    def build(h):
        lane = lax.broadcasted_iota(jnp.int32, (bases.shape[2], width), 1)
        row = lax.broadcasted_iota(jnp.int32, (bases.shape[2], width), 0)
        wide = jnp.where(lax.div(lane, side) == row, 1.0, 0.0).astype(BF16)
        tiled = jnp.where(lax.rem(lane, side) + side == row, 1.0, 0.0).astype(BF16)
        outer = jnp.dot(bases[h], wide, preferred_element_type=F32)
        inner = jnp.dot(bases[h], tiled, preferred_element_type=F32)
        for a in range(side):
            rot[h, pl.ds(a * side, side), :] = (outer[a : a + 1] * inner).astype(BF16)

    build(zh)

    for h in range(zh_n):
        gathered[h, pl.ds(pl.multiple_of(ti * rows, rows), rows)] = ordered[h * t_n + ti]

    crossed[xi] = query_ref[...]

    @pl.loop(1, x_n)
    def _(i):
        x = lax.rem(xi + i, x_n)
        remote(query_ref, crossed.at[x], s1s.at[x], s1r.at[x], at()).wait_recv()

    offer[...] = crossed[lax.rem(owner_ref[xi], x_n)]
    for step in range(min(2, steps), steps):
        hear(step)

    def span_of(z):
        return pl.ds(pl.multiple_of(z * piece, piece), piece)

    def send2(z):
        return remote(
            offer.at[:, span_of(z)], offered.at[zl], s2s.at[z], s2r.at[zl], at(z=zh * zl_n + z)
        )

    @pl.loop(1, zl_n)
    def _(i):
        send2(lax.rem(zl + i, zl_n)).start()

    other = zh_n - 1 - zh
    twins = [
        remote(bases.at[zh], bases.at[zh], sbs.at[0], sbr.at[0], at(z=z_n - 1 - zi)),
        remote(eigs.at[zh], eigs.at[zh], sbs.at[1], sbr.at[1], at(z=z_n - 1 - zi)),
    ]
    for twin in twins:
        twin.start()

    offered[zl] = offer[:, span_of(zl)]

    @pl.loop(1, zl_n)
    def _(i):
        z = lax.rem(zl + i, zl_n)
        remote(offered.at[z], offered.at[z], s2s.at[z], s2r.at[z], at()).wait_recv()

    lines = pl.ds(pl.multiple_of(xi * held, held), held)
    chosen[zh, lines, span_of(zl)] = offered[lax.div(owner_ref[xi], x_n)]

    def chunk(z, k):
        return chosen.at[
            lax.div(z, zl_n),
            pl.ds(pl.multiple_of(k * held, held), held),
            pl.ds(pl.multiple_of(lax.rem(z, zl_n) * piece, piece), piece),
        ]

    def send3(z):
        return remote(chunk(zi, xi), chunk(zi, xi), s3s.at[z], s3r.at[zi], at(z=z))

    @pl.loop(1, z_n)
    def _(i):
        send3(lax.rem(zi + i, z_n)).start()

    for twin in twins:
        twin.wait_send()
    for i, buf in enumerate((bases, eigs)):
        remote(buf.at[other], buf.at[other], sbs.at[i], sbr.at[i], at()).wait_recv()
    build(other)

    def turn(y):
        @pl.loop(0, zh_n)
        def _(h):
            some = pl.ds(pl.multiple_of(y * c_n * rows, c_n * rows), c_n * rows)
            turned[h, some, :] = jnp.dot(
                gathered[h, some, :], rot[h], preferred_element_type=F32
            ).astype(BF16)

    sibling = jnp.bitwise_xor(ti, 1)
    for h in range(zh_n):
        got_g(sibling, h).wait_recv()
    turn(yi)
    total_asked[...] = jnp.zeros_like(total_asked)

    quarters = s4s.shape[1]
    each = z_n // quarters

    def quarter(q, k):
        per = quarters // zh_n
        return chosen.at[
            lax.div(q, per),
            pl.ds(pl.multiple_of(k * held, held), held),
            pl.ds(pl.multiple_of(lax.rem(q, per) * each * piece, each * piece), each * piece),
        ]

    def send4(x, q):
        return remote(quarter(q, xi), quarter(q, xi), s4s.at[x, q], s4r.at[xi, q], at(x=x))

    home = lax.div(zi, each)
    order = [lax.rem(home + j, quarters) for j in (0, 1, quarters - 1, 2)]
    for q in order:

        @pl.loop(0, each)
        def _(i):
            z = q * each + i

            @pl.when(z != zi)
            def _():
                remote(chunk(z, xi), chunk(z, xi), s3s.at[z], s3r.at[z], at()).wait_recv()

        @pl.loop(1, x_n)
        def _(i):
            send4(lax.rem(xi + i, x_n), q).start()

    def await_g(y):
        for c in range(c_n):
            for h in range(zh_n):
                got_g(y * c_n + c, h).wait_recv()

    for j in near:
        await_g(jnp.bitwise_xor(yi, j))
        turn(jnp.bitwise_xor(yi, j))

    half = each * piece
    for q in order:

        @pl.loop(1, x_n)
        def _(i):
            x = lax.rem(xi + i, x_n)
            remote(quarter(q, x), quarter(q, x), s4s.at[x, q], s4r.at[x, q], at()).wait_recv()

        h = lax.div(q, quarters // zh_n)
        these = pl.ds(pl.multiple_of(lax.rem(q, quarters // zh_n) * half, half), half)
        total_asked[h] += jnp.dot(
            chosen[h, :, these], rot[h, these, :], preferred_element_type=F32
        )

    for h in range(zh_n):
        damping = 0.1 * jnp.mean(eigs[h], axis=1, keepdims=True)
        asked[h] = (total_asked[h] / (eigs[h] + damping)).astype(BF16)

    def score(y):
        some = pl.ds(pl.multiple_of(y * c_n * rows, c_n * rows), c_n * rows)
        total = None
        for h in range(zh_n):
            term = lax.dot_general(
                turned[h, some, :], asked[h], (((1,), (1,)), ((), ())), preferred_element_type=F32
            )
            total = term if total is None else total + term
        part[pl.ds(y * c_n, c_n)] = total.reshape(c_n, rows, total.shape[1]).astype(BF16)
        return total

    def send_p(t):
        return remote(part.at[t], parts.at[ti], sps.at[t], spr.at[ti], at(t=t))

    for j in near + far + [0]:
        y = jnp.bitwise_xor(yi, j)
        if j in far:
            await_g(y)
            turn(y)
        total = score(y)
        for c in range(c_n):
            if j:
                send_p(y * c_n + c).start()
        if j == 0:
            send_p(sibling).start()
            whole[...] = total.reshape(c_n, rows, total.shape[1])

    @pl.loop(1, zl_n)
    def _(i):
        send2(lax.rem(zl + i, zl_n)).wait_send()

    @pl.loop(1, z_n)
    def _(i):
        send3(lax.rem(zi + i, z_n)).wait_send()

    @pl.loop(1, x_n)
    def _(i):
        x = lax.rem(xi + i, x_n)
        send1(x).wait_send()
        for q in range(quarters):
            send4(x, q).wait_send()

    @pl.loop(1, t_n)
    def _(i):
        for h in range(zh_n):
            send_g(jnp.bitwise_xor(ti, i), h).wait_send()

    @pl.loop(1, t_n)
    def _(i):
        t = jnp.bitwise_xor(ti, i)
        remote(parts.at[t], parts.at[t], sps.at[t], spr.at[t], at()).wait_recv()

    total = whole[lax.rem(ti, c_n)]
    for i in range(1, t_n):
        total += parts[jnp.bitwise_xor(ti, i)].astype(F32)
    out_ref[...] = total * (1.0 / math.sqrt(modules * width))

    @pl.loop(1, t_n)
    def _(i):
        send_p(jnp.bitwise_xor(ti, i)).wait_send()


def local(dims, train_grads, query_grads, basis_out, basis_in, eigenvalues, owner_groups, module_order):
    zl_n, x_n, zh_n, y_n, c_n = dims
    rows, modules, width = train_grads.shape
    held, side = query_grads.shape[1], basis_out.shape[1]
    t_n, z_n, piece = y_n * c_n, zh_n * zl_n, width // zl_n
    asks = owner_groups.shape[0] * held
    dma = pltpu.SemaphoreType.DMA
    return pl.pallas_call(
        functools.partial(kernel, dims),
        out_shape=jax.ShapeDtypeStruct((rows, asks), F32),
        in_specs=[pl.BlockSpec(memory_space=pl.ANY)] * 7,
        out_specs=pl.BlockSpec(memory_space=pltpu.VMEM),
        scratch_shapes=[
            pltpu.VMEM((rows, modules, width), BF16),
            pltpu.VMEM((held, width), BF16),
            pltpu.VMEM((side, side), BF16),
            pltpu.VMEM((side, side), BF16),
            pltpu.SMEM(owner_groups.shape, jnp.int32),
            pltpu.SMEM(module_order.shape, jnp.int32),
            dma((7,)),
            pltpu.VMEM((16 * modules, 16 * modules), BF16),
            pltpu.VMEM((modules, rows, width), BF16),
            pltpu.VMEM((zh_n, t_n * rows, width), BF16),
            pltpu.VMEM((zh_n, width, width), BF16),
            pltpu.VMEM((zh_n, t_n * rows, width), BF16),
            pltpu.VMEM((zh_n, side, 128), BF16),
            pltpu.VMEM((zh_n, 1, width), F32),
            pltpu.SemaphoreType.REGULAR(((z_n // 2).bit_length() - 1,)),
            pltpu.VMEM((x_n, held, width), BF16),
            pltpu.VMEM((held, width), BF16),
            pltpu.VMEM((zl_n, held, piece), BF16),
            pltpu.VMEM((zh_n, asks, width), BF16),
            pltpu.VMEM((zh_n, asks, width), BF16),
            pltpu.VMEM((zh_n, asks, width), F32),
            pltpu.VMEM((t_n, rows, asks), BF16),
            pltpu.VMEM((t_n, rows, asks), BF16),
            pltpu.VMEM((c_n, rows, asks), F32),
            dma((x_n,)),
            dma((x_n,)),
            dma((zl_n,)),
            dma((zl_n,)),
            dma((z_n,)),
            dma((z_n,)),
            dma((x_n, 4)),
            dma((x_n, 4)),
            dma((t_n, zh_n)),
            dma((t_n, zh_n)),
            dma((2,)),
            dma((2,)),
            dma((t_n,)),
            dma((t_n,)),
        ],
        compiler_params=pltpu.CompilerParams(
            collective_id=0, has_side_effects=True, vmem_limit_bytes=60 << 20
        ),
    )(
        train_grads,
        query_grads.reshape(held, width),
        basis_out[0],
        basis_in[0],
        eigenvalues,
        owner_groups,
        module_order,
    )


def solution(mesh, layout=(X, ZH, Y, C)):
    x_n, zh_n, y_n, c_n = layout
    dims = (mesh.shape["group"] // x_n, x_n, zh_n, y_n, c_n)
    in_specs = (
        P(("group", "module"), None, None),
        P("group", None, "module", None),
        P("module", None, None),
        P("module", None, None),
        P("module", None),
        P(),
        P(),
    )
    out_specs = P(("group", "module"), None)
    return jax.shard_map(
        functools.partial(local, dims), mesh=mesh, in_specs=in_specs, out_specs=out_specs, check_vma=False
    )
```

```python
import functools
import math

import jax
import jax.numpy as jnp
from jax import lax
from jax.experimental import pallas as pl
from jax.experimental.pallas import tpu as pltpu
from jax.sharding import PartitionSpec as P

ZH, Y, C = 2, 4, 2
X = 4
F32, BF16 = jnp.float32, jnp.bfloat16


def kernel(
    dims,
    train_hbm,
    query_hbm,
    bout_hbm,
    bin_hbm,
    eig_hbm,
    owner_hbm,
    order_hbm,
    out_ref,
    train_ref,
    query_ref,
    bout_ref,
    bin_ref,
    owner_ref,
    order_ref,
    fetch_sem,
    perm,
    ordered,
    gathered,
    rot,
    turned,
    bases,
    eigs,
    heard,
    crossed,
    offer,
    offered,
    chosen,
    asked,
    divisor,
    part,
    parts,
    whole,
    s1s,
    s1r,
    s2s,
    s2r,
    s3s,
    s3r,
    s4s,
    s4r,
    sgs,
    sgr,
    sbs,
    sbr,
    sps,
    spr,
):
    zl_n, x_n, zh_n, y_n, c_n = dims
    t_n = y_n * c_n
    z_n = zh_n * zl_n
    rows, modules, width = train_ref.shape
    held = query_ref.shape[0]
    owners = owner_hbm.shape[0]
    per = zl_n // owners
    wide_x = width // x_n
    piece = wide_x // per
    group, module = lax.axis_index("group"), lax.axis_index("module")
    zl, xi = lax.div(group, x_n), lax.rem(group, x_n)
    zh, ti = lax.div(module, t_n), lax.rem(module, t_n)
    yi = lax.div(ti, c_n)
    zi = zh * zl_n + zl

    def at(z=None, x=None, t=None):
        z = zi if z is None else z
        x = xi if x is None else x
        t = ti if t is None else t
        return (lax.rem(z, zl_n) * x_n + x, lax.div(z, zl_n) * t_n + t)

    def remote(src, dst, send, recv, where):
        return pltpu.make_async_remote_copy(
            src_ref=src,
            dst_ref=dst,
            send_sem=send,
            recv_sem=recv,
            device_id=where,
            device_id_type=pl.DeviceIdType.MESH,
        )

    fetches = [
        pltpu.make_async_copy(src, dst, fetch_sem.at[i])
        for i, (src, dst) in enumerate(
            (
                (order_hbm, order_ref),
                (train_hbm, train_ref),
                (query_hbm, query_ref),
                (bout_hbm, bout_ref),
                (bin_hbm, bin_ref),
                (eig_hbm, eigs.at[zh]),
                (owner_hbm, owner_ref),
            )
        )
    ]
    for fetch in fetches:
        fetch.start()

    barrier = pltpu.get_barrier_semaphore()

    def greet(where):
        pl.semaphore_signal(
            barrier, inc=1, device_id=where, device_id_type=pl.DeviceIdType.MESH
        )

    around = sorted({1, 2, z_n - 2, z_n - 1})
    for i in around:
        greet(at(z=lax.rem(zi + i, z_n)))

    @pl.loop(1, x_n)
    def _(i):
        greet(at(x=lax.rem(xi + i, x_n)))

    @pl.loop(1, t_n)
    def _(i):
        greet(at(t=lax.rem(ti + i, t_n)))

    order_in, train_in, query_in, *small_in = fetches
    query_in.wait()
    pl.semaphore_wait(barrier, len(around) + x_n + t_n - 2)

    def columns_of(x):
        return pl.ds(pl.multiple_of(x * wide_x, wide_x), wide_x)

    def send1(x):
        return remote(
            query_ref.at[:, columns_of(x)], crossed.at[xi], s1s.at[x], s1r.at[xi], at(x=x)
        )

    @pl.loop(1, x_n)
    def _(i):
        send1(lax.rem(xi + i, x_n)).start()

    def tell(step):
        d = 2 << step
        for z in (lax.rem(zi + d, z_n), lax.rem(zi + z_n - d, z_n)):
            pl.semaphore_signal(
                heard.at[step], inc=1, device_id=at(z=z), device_id_type=pl.DeviceIdType.MESH
            )

    def hear(step):
        pl.semaphore_wait(heard.at[step], 2)
        if step + 1 < steps:
            tell(step + 1)

    steps = (z_n // 2).bit_length() - 2
    if steps:
        tell(0)

    batch = 16
    span = batch * modules
    order_in.wait()
    for s in range(modules):
        lane = lax.broadcasted_iota(jnp.int32, (batch, span), 1)
        row = lax.broadcasted_iota(jnp.int32, (batch, span), 0)
        hit = lane == row * modules + order_ref[s]
        perm[pl.ds(s * batch, batch), :] = jnp.where(hit, 1.0, 0.0).astype(BF16)
    train_in.wait()
    for b in range(rows // batch):
        block = train_ref[pl.ds(b * batch, batch)].reshape(span, width)
        moved = jnp.dot(perm[...], block, preferred_element_type=F32).astype(BF16)
        ordered[:, pl.ds(b * batch, batch), :] = moved.reshape(modules, batch, width)
    if steps:
        hear(0)

    def send_g(t, h):
        return remote(
            ordered.at[h * t_n + t],
            gathered.at[h, pl.ds(pl.multiple_of(ti * rows, rows), rows)],
            sgs.at[t, h],
            sgr.at[ti, h],
            at(t=t),
        )

    def got_g(t, h):
        return remote(
            ordered.at[h * t_n + t],
            gathered.at[h, pl.ds(pl.multiple_of(t * rows, rows), rows)],
            sgs.at[t, h],
            sgr.at[t, h],
            at(t=t),
        )

    near = [j for j in range(1, y_n) if j != 2]
    far = [j for j in range(1, y_n) if j == 2]
    for j in [0] + near + far:
        for h in range(zh_n):
            for c in range(1 if j == 0 else 0, c_n):
                send_g(jnp.bitwise_xor(ti, j * c_n + c), h).start()

    for fetch in small_in:
        fetch.wait()

    bases[zh] = jnp.zeros(bases.shape[1:], BF16)
    side = bout_ref.shape[1]
    bases[zh, :, :side] = bout_ref[...]
    bases[zh, :, side : 2 * side] = bin_ref[...]

    def build(h):
        lane = lax.broadcasted_iota(jnp.int32, (bases.shape[2], width), 1)
        row = lax.broadcasted_iota(jnp.int32, (bases.shape[2], width), 0)
        wide = jnp.where(lax.div(lane, side) == row, 1.0, 0.0).astype(BF16)
        tiled = jnp.where(lax.rem(lane, side) + side == row, 1.0, 0.0).astype(BF16)
        outer = jnp.dot(bases[h], wide, preferred_element_type=F32)
        inner = jnp.dot(bases[h], tiled, preferred_element_type=F32)
        for a in range(side):
            rot[h, pl.ds(a * side, side), :] = (outer[a : a + 1] * inner).astype(BF16)

    build(zh)

    for h in range(zh_n):
        gathered[h, pl.ds(pl.multiple_of(ti * rows, rows), rows)] = ordered[h * t_n + ti]

    crossed[xi] = query_ref[:, columns_of(xi)]

    @pl.loop(1, x_n)
    def _(i):
        x = lax.rem(xi + i, x_n)
        remote(crossed.at[x], crossed.at[x], s1s.at[x], s1r.at[x], at()).wait_recv()

    for k in range(owners):
        offer[k] = crossed[lax.rem(owner_ref[k], x_n)]
    for step in range(1, steps):
        hear(step)

    def lines_of(k, n=1):
        return pl.ds(pl.multiple_of(k * held, n * held), n * held)

    def send2(z):
        part_z = pl.ds(pl.multiple_of(lax.rem(z, per) * piece, piece), piece)
        return remote(
            offer.at[lax.div(z, per), :, part_z],
            offered.at[zl],
            s2s.at[z],
            s2r.at[zl],
            at(z=zh * zl_n + z),
        )

    @pl.loop(1, zl_n)
    def _(i):
        send2(lax.rem(zl + i, zl_n)).start()

    other = zh_n - 1 - zh
    twins = [
        remote(bases.at[zh], bases.at[zh], sbs.at[0], sbr.at[0], at(z=z_n - 1 - zi)),
        remote(eigs.at[zh], eigs.at[zh], sbs.at[1], sbr.at[1], at(z=z_n - 1 - zi)),
    ]
    for twin in twins:
        twin.start()

    mine = lax.div(zl, per)
    offered[zl] = offer[mine, :, pl.ds(pl.multiple_of(lax.rem(zl, per) * piece, piece), piece)]

    @pl.loop(1, zl_n)
    def _(i):
        z = lax.rem(zl + i, zl_n)
        remote(offered.at[z], offered.at[z], s2s.at[z], s2r.at[z], at()).wait_recv()

    def place(z, x):
        zz = lax.rem(z, zl_n)
        start = x * wide_x + lax.rem(zz, per) * piece
        return (
            lax.div(z, zl_n),
            lines_of(lax.div(zz, per)),
            pl.ds(pl.multiple_of(start, piece), piece),
        )

    def chunk(z, x):
        return chosen.at[place(z, x)]

    chosen[place(zi, xi)] = offered[lax.div(owner_ref[mine], x_n)]

    def send3(z):
        return remote(chunk(zi, xi), chunk(zi, xi), s3s.at[z], s3r.at[zi], at(z=z))

    @pl.loop(1, z_n)
    def _(i):
        send3(lax.rem(zi + i, z_n)).start()

    for twin in twins:
        twin.wait_send()
    for i, buf in enumerate((bases, eigs)):
        remote(buf.at[other], buf.at[other], sbs.at[i], sbr.at[i], at()).wait_recv()
    build(other)

    def turn_slot(y, h):
        some = pl.ds(pl.multiple_of(y * c_n * rows, c_n * rows), c_n * rows)
        turned[h, some, :] = jnp.dot(
            gathered[h, some, :], rot[h], preferred_element_type=F32
        ).astype(BF16)

    sibling = jnp.bitwise_xor(ti, 1)
    for h in range(zh_n):
        got_g(sibling, h).wait_recv()

    @pl.loop(0, zh_n)
    def _(h):
        turn_slot(yi, h)

    for h in range(zh_n):
        divisor[h] = eigs[h] + 0.1 * jnp.mean(eigs[h], axis=1, keepdims=True)

    def block(e, x):
        return chosen.at[lax.div(e, owners), lines_of(lax.rem(e, owners)), columns_of(x)]

    def send4(x, e):
        return remote(block(e, xi), block(e, xi), s4s.at[x, e], s4r.at[xi, e], at(x=x))

    blocks = s4s.shape[1]
    quarters = blocks // 2
    home = lax.div(zi, 2 * per)
    nearest = (0, 1, 3, 2) if quarters == 4 else range(quarters)
    order = [lax.rem(home + j, quarters) for j in nearest]
    for q in order:

        @pl.loop(2 * q, 2 * q + 2)
        def _(e):
            for i in range(per):
                z = e * per + i

                @pl.when(z != zi)
                def _():
                    remote(chunk(z, xi), chunk(z, xi), s3s.at[z], s3r.at[z], at()).wait_recv()

            for i in range(1, x_n):
                send4(lax.rem(xi + i, x_n), e).start()

    def turn_got(y):
        @pl.loop(0, zh_n)
        def _(h):
            for c in range(c_n):
                got_g(y * c_n + c, h).wait_recv()
            turn_slot(y, h)

    for j in near:
        turn_got(jnp.bitwise_xor(yi, j))

    for q in order:
        for e in (2 * q, 2 * q + 1):
            for i in range(1, x_n):
                x = lax.rem(xi + i, x_n)
                remote(block(e, x), block(e, x), s4s.at[x, e], s4r.at[x, e], at()).wait_recv()
        h = lax.div(2 * q, owners)
        these = lines_of(lax.rem(2 * q, owners), 2)
        product = jnp.dot(chosen[h, these, :], rot[h], preferred_element_type=F32)
        asked[h, these, :] = (product / divisor[h]).astype(BF16)

    def score(y):
        some = pl.ds(pl.multiple_of(y * c_n * rows, c_n * rows), c_n * rows)
        total = None
        for h in range(zh_n):
            term = lax.dot_general(
                turned[h, some, :], asked[h], (((1,), (1,)), ((), ())), preferred_element_type=F32
            )
            total = term if total is None else total + term
        part[pl.ds(y * c_n, c_n)] = total.reshape(c_n, rows, total.shape[1]).astype(BF16)
        return total

    def send_p(t):
        return remote(part.at[t], parts.at[ti], sps.at[t], spr.at[ti], at(t=t))

    for j in near + far + [0]:
        y = jnp.bitwise_xor(yi, j)
        if j in far:
            turn_got(y)
        total = score(y)
        for c in range(c_n):
            if j:
                send_p(y * c_n + c).start()
        if j == 0:
            send_p(sibling).start()
            whole[...] = total.reshape(c_n, rows, total.shape[1])

    @pl.loop(1, zl_n)
    def _(i):
        send2(lax.rem(zl + i, zl_n)).wait_send()

    @pl.loop(1, z_n)
    def _(i):
        send3(lax.rem(zi + i, z_n)).wait_send()

    @pl.loop(1, x_n)
    def _(i):
        x = lax.rem(xi + i, x_n)
        send1(x).wait_send()
        for e in range(blocks):
            send4(x, e).wait_send()

    @pl.loop(1, t_n)
    def _(i):
        for h in range(zh_n):
            send_g(jnp.bitwise_xor(ti, i), h).wait_send()

    @pl.loop(1, t_n)
    def _(i):
        t = jnp.bitwise_xor(ti, i)
        remote(parts.at[t], parts.at[t], sps.at[t], spr.at[t], at()).wait_recv()

    total = whole[lax.rem(ti, c_n)]
    for i in range(1, t_n):
        total += parts[jnp.bitwise_xor(ti, i)].astype(F32)
    out_ref[...] = total * (1.0 / math.sqrt(modules * width))

    @pl.loop(1, t_n)
    def _(i):
        send_p(jnp.bitwise_xor(ti, i)).wait_send()


def local(dims, train_grads, query_grads, basis_out, basis_in, eigenvalues, owner_groups, module_order):
    zl_n, x_n, zh_n, y_n, c_n = dims
    rows, modules, width = train_grads.shape
    held, side = query_grads.shape[1], basis_out.shape[1]
    t_n, z_n, owners = y_n * c_n, zh_n * zl_n, owner_groups.shape[0]
    asks, wide_x, piece = owners * held, width // x_n, width // x_n // (zl_n // owners)
    dma = pltpu.SemaphoreType.DMA
    return pl.pallas_call(
        functools.partial(kernel, dims),
        out_shape=jax.ShapeDtypeStruct((rows, asks), F32),
        in_specs=[pl.BlockSpec(memory_space=pl.ANY)] * 7,
        out_specs=pl.BlockSpec(memory_space=pltpu.VMEM),
        scratch_shapes=[
            pltpu.VMEM((rows, modules, width), BF16),
            pltpu.VMEM((held, width), BF16),
            pltpu.VMEM((side, side), BF16),
            pltpu.VMEM((side, side), BF16),
            pltpu.SMEM(owner_groups.shape, jnp.int32),
            pltpu.SMEM(module_order.shape, jnp.int32),
            dma((7,)),
            pltpu.VMEM((16 * modules, 16 * modules), BF16),
            pltpu.VMEM((modules, rows, width), BF16),
            pltpu.VMEM((zh_n, t_n * rows, width), BF16),
            pltpu.VMEM((zh_n, width, width), BF16),
            pltpu.VMEM((zh_n, t_n * rows, width), BF16),
            pltpu.VMEM((zh_n, side, 128), BF16),
            pltpu.VMEM((zh_n, 1, width), F32),
            pltpu.SemaphoreType.REGULAR((max(1, (z_n // 2).bit_length() - 2),)),
            pltpu.VMEM((x_n, held, wide_x), BF16),
            pltpu.VMEM((owners, held, wide_x), BF16),
            pltpu.VMEM((zl_n, held, piece), BF16),
            pltpu.VMEM((zh_n, asks, width), BF16),
            pltpu.VMEM((zh_n, asks, width), BF16),
            pltpu.VMEM((zh_n, 1, width), F32),
            pltpu.VMEM((t_n, rows, asks), BF16),
            pltpu.VMEM((t_n, rows, asks), BF16),
            pltpu.VMEM((c_n, rows, asks), F32),
            dma((x_n,)),
            dma((x_n,)),
            dma((zl_n,)),
            dma((zl_n,)),
            dma((z_n,)),
            dma((z_n,)),
            dma((x_n, zh_n * owners)),
            dma((x_n, zh_n * owners)),
            dma((t_n, zh_n)),
            dma((t_n, zh_n)),
            dma((2,)),
            dma((2,)),
            dma((t_n,)),
            dma((t_n,)),
        ],
        compiler_params=pltpu.CompilerParams(
            collective_id=0, has_side_effects=True, vmem_limit_bytes=60 << 20
        ),
    )(
        train_grads,
        query_grads.reshape(held, width),
        basis_out[0],
        basis_in[0],
        eigenvalues,
        owner_groups,
        module_order,
    )


def solution(mesh, layout=(X, ZH, Y, C)):
    x_n, zh_n, y_n, c_n = layout
    dims = (mesh.shape["group"] // x_n, x_n, zh_n, y_n, c_n)
    in_specs = (
        P(("group", "module"), None, None),
        P("group", None, "module", None),
        P("module", None, None),
        P("module", None, None),
        P("module", None),
        P(),
        P(),
    )
    out_specs = P(("group", "module"), None)
    return jax.shard_map(
        functools.partial(local, dims), mesh=mesh, in_specs=in_specs, out_specs=out_specs, check_vma=False
    )
```

```python
import functools
import math

import jax
import jax.numpy as jnp
from jax import lax
from jax.experimental import pallas as pl
from jax.experimental.pallas import tpu as pltpu
from jax.sharding import PartitionSpec as P

ZH, Y, C = 2, 4, 2
X = 4
F32, BF16 = jnp.float32, jnp.bfloat16


def kernel(
    dims,
    train_hbm,
    query_hbm,
    bout_hbm,
    bin_hbm,
    eig_hbm,
    owner_hbm,
    order_hbm,
    out_ref,
    train_ref,
    query_ref,
    bout_ref,
    bin_ref,
    owner_ref,
    order_ref,
    fetch_sem,
    perm,
    ordered,
    gathered,
    rot,
    turned,
    bases,
    eigs,
    heard,
    crossed,
    offer,
    offered,
    chosen,
    asked,
    divisor,
    part,
    parts,
    whole,
    s1s,
    s1r,
    s2s,
    s2r,
    s3s,
    s3r,
    s4s,
    s4r,
    sgs,
    sgr,
    sbs,
    sbr,
    sps,
    spr,
):
    zl_n, x_n, zh_n, y_n, c_n = dims
    t_n = y_n * c_n
    z_n = zh_n * zl_n
    rows, modules, width = train_ref.shape
    held = query_ref.shape[0]
    owners = owner_hbm.shape[0]
    per = zl_n // owners
    wide_x = width // x_n
    piece = wide_x // per
    group, module = lax.axis_index("group"), lax.axis_index("module")
    zl, xi = lax.div(group, x_n), lax.rem(group, x_n)
    zh, ti = lax.div(module, t_n), lax.rem(module, t_n)
    yi = lax.div(ti, c_n)
    zi = zh * zl_n + zl

    def at(z=None, x=None, t=None):
        z = zi if z is None else z
        x = xi if x is None else x
        t = ti if t is None else t
        return (lax.rem(z, zl_n) * x_n + x, lax.div(z, zl_n) * t_n + t)

    def remote(src, dst, send, recv, where):
        return pltpu.make_async_remote_copy(
            src_ref=src,
            dst_ref=dst,
            send_sem=send,
            recv_sem=recv,
            device_id=where,
            device_id_type=pl.DeviceIdType.MESH,
        )

    fetches = [
        pltpu.make_async_copy(src, dst, fetch_sem.at[i])
        for i, (src, dst) in enumerate(
            (
                (order_hbm, order_ref),
                (train_hbm, train_ref),
                (query_hbm, query_ref),
                (bout_hbm, bout_ref),
                (bin_hbm, bin_ref),
                (eig_hbm, eigs.at[zh]),
                (owner_hbm, owner_ref),
            )
        )
    ]
    for fetch in fetches:
        fetch.start()

    barrier = pltpu.get_barrier_semaphore()

    def greet(where):
        pl.semaphore_signal(
            barrier, inc=1, device_id=where, device_id_type=pl.DeviceIdType.MESH
        )

    around = sorted({1, 2, z_n - 2, z_n - 1})
    for i in around:
        greet(at(z=lax.rem(zi + i, z_n)))

    @pl.loop(1, x_n)
    def _(i):
        greet(at(x=lax.rem(xi + i, x_n)))

    @pl.loop(1, t_n)
    def _(i):
        greet(at(t=lax.rem(ti + i, t_n)))

    order_in, train_in, query_in, *small_in = fetches

    batch = 16
    span = batch * modules
    order_in.wait()
    for s in range(modules):
        lane = lax.broadcasted_iota(jnp.int32, (batch, span), 1)
        row = lax.broadcasted_iota(jnp.int32, (batch, span), 0)
        hit = lane == row * modules + order_ref[s]
        perm[pl.ds(s * batch, batch), :] = jnp.where(hit, 1.0, 0.0).astype(BF16)
    train_in.wait()
    for b in range(rows // batch):
        block = train_ref[pl.ds(b * batch, batch)].reshape(span, width)
        moved = jnp.dot(perm[...], block, preferred_element_type=F32).astype(BF16)
        ordered[:, pl.ds(b * batch, batch), :] = moved.reshape(modules, batch, width)
    query_in.wait()
    pl.semaphore_wait(barrier, len(around) + x_n + t_n - 2)

    def columns_of(x):
        return pl.ds(pl.multiple_of(x * wide_x, wide_x), wide_x)

    def send1(x):
        return remote(
            query_ref.at[:, columns_of(x)], crossed.at[xi], s1s.at[x], s1r.at[xi], at(x=x)
        )

    @pl.loop(1, x_n)
    def _(i):
        send1(lax.rem(xi + i, x_n)).start()

    def tell(step):
        d = 2 << step
        for z in (lax.rem(zi + d, z_n), lax.rem(zi + z_n - d, z_n)):
            pl.semaphore_signal(
                heard.at[step], inc=1, device_id=at(z=z), device_id_type=pl.DeviceIdType.MESH
            )

    def hear(step):
        pl.semaphore_wait(heard.at[step], 2)
        if step + 1 < steps:
            tell(step + 1)

    steps = (z_n // 2).bit_length() - 2
    if steps:
        tell(0)

    def send_g(t, h):
        return remote(
            ordered.at[h * t_n + t],
            gathered.at[h, pl.ds(pl.multiple_of(ti * rows, rows), rows)],
            sgs.at[t, h],
            sgr.at[ti, h],
            at(t=t),
        )

    def got_g(t, h):
        return remote(
            ordered.at[h * t_n + t],
            gathered.at[h, pl.ds(pl.multiple_of(t * rows, rows), rows)],
            sgs.at[t, h],
            sgr.at[t, h],
            at(t=t),
        )

    near = [j for j in range(1, y_n) if j != 2]
    far = [j for j in range(1, y_n) if j == 2]
    for j in [0] + near + far:
        for h in range(zh_n):
            for c in range(1 if j == 0 else 0, c_n):
                send_g(jnp.bitwise_xor(ti, j * c_n + c), h).start()

    if steps:
        hear(0)
    for fetch in small_in:
        fetch.wait()

    bases[zh] = jnp.zeros(bases.shape[1:], BF16)
    side = bout_ref.shape[1]
    bases[zh, :, :side] = bout_ref[...]
    bases[zh, :, side : 2 * side] = bin_ref[...]

    def build(h):
        lane = lax.broadcasted_iota(jnp.int32, (bases.shape[2], width), 1)
        row = lax.broadcasted_iota(jnp.int32, (bases.shape[2], width), 0)
        wide = jnp.where(lax.div(lane, side) == row, 1.0, 0.0).astype(BF16)
        tiled = jnp.where(lax.rem(lane, side) + side == row, 1.0, 0.0).astype(BF16)
        outer = jnp.dot(bases[h], wide, preferred_element_type=F32)
        inner = jnp.dot(bases[h], tiled, preferred_element_type=F32)
        for a in range(side):
            rot[h, pl.ds(a * side, side), :] = (outer[a : a + 1] * inner).astype(BF16)

    build(zh)

    for h in range(zh_n):
        gathered[h, pl.ds(pl.multiple_of(ti * rows, rows), rows)] = ordered[h * t_n + ti]

    crossed[xi] = query_ref[:, columns_of(xi)]

    @pl.loop(1, x_n)
    def _(i):
        x = lax.rem(xi + i, x_n)
        remote(crossed.at[x], crossed.at[x], s1s.at[x], s1r.at[x], at()).wait_recv()

    for k in range(owners):
        offer[k] = crossed[lax.rem(owner_ref[k], x_n)]
    for step in range(1, steps):
        hear(step)

    def lines_of(k, n=1):
        return pl.ds(pl.multiple_of(k * held, n * held), n * held)

    def send2(z):
        part_z = pl.ds(pl.multiple_of(lax.rem(z, per) * piece, piece), piece)
        return remote(
            offer.at[lax.div(z, per), :, part_z],
            offered.at[zl],
            s2s.at[z],
            s2r.at[zl],
            at(z=zh * zl_n + z),
        )

    @pl.loop(1, zl_n)
    def _(i):
        send2(lax.rem(zl + i, zl_n)).start()

    other = zh_n - 1 - zh
    twins = [
        remote(bases.at[zh], bases.at[zh], sbs.at[0], sbr.at[0], at(z=z_n - 1 - zi)),
        remote(eigs.at[zh], eigs.at[zh], sbs.at[1], sbr.at[1], at(z=z_n - 1 - zi)),
    ]
    for twin in twins:
        twin.start()

    mine = lax.div(zl, per)
    offered[zl] = offer[mine, :, pl.ds(pl.multiple_of(lax.rem(zl, per) * piece, piece), piece)]

    @pl.loop(1, zl_n)
    def _(i):
        z = lax.rem(zl + i, zl_n)
        remote(offered.at[z], offered.at[z], s2s.at[z], s2r.at[z], at()).wait_recv()

    def place(z, x):
        zz = lax.rem(z, zl_n)
        start = x * wide_x + lax.rem(zz, per) * piece
        return (
            lax.div(z, zl_n),
            lines_of(lax.div(zz, per)),
            pl.ds(pl.multiple_of(start, piece), piece),
        )

    def chunk(z, x):
        return chosen.at[place(z, x)]

    chosen[place(zi, xi)] = offered[lax.div(owner_ref[mine], x_n)]

    def send3(z):
        return remote(chunk(zi, xi), chunk(zi, xi), s3s.at[z], s3r.at[zi], at(z=z))

    send3(lax.rem(zi + z_n // 2, z_n)).start()

    @pl.loop(1, z_n // 2)
    def _(i):
        send3(lax.rem(zi + z_n // 2 - i, z_n)).start()
        send3(lax.rem(zi + z_n // 2 + i, z_n)).start()

    for twin in twins:
        twin.wait_send()
    for i, buf in enumerate((bases, eigs)):
        remote(buf.at[other], buf.at[other], sbs.at[i], sbr.at[i], at()).wait_recv()
    build(other)

    def turn_slot(y, h):
        some = pl.ds(pl.multiple_of(y * c_n * rows, c_n * rows), c_n * rows)
        turned[h, some, :] = jnp.dot(
            gathered[h, some, :], rot[h], preferred_element_type=F32
        ).astype(BF16)

    sibling = jnp.bitwise_xor(ti, 1)
    for h in range(zh_n):
        got_g(sibling, h).wait_recv()

    @pl.loop(0, zh_n)
    def _(h):
        turn_slot(yi, h)

    for h in range(zh_n):
        divisor[h] = eigs[h] + 0.1 * jnp.mean(eigs[h], axis=1, keepdims=True)

    def block(e, x):
        return chosen.at[lax.div(e, owners), lines_of(lax.rem(e, owners)), columns_of(x)]

    def send4(x, e):
        return remote(block(e, xi), block(e, xi), s4s.at[x, e], s4r.at[xi, e], at(x=x))

    blocks = s4s.shape[1]
    quarters = blocks // 2
    home = lax.div(zi, 2 * per)
    nearest = (0, 1, 3, 2) if quarters == 4 else range(quarters)
    order = [lax.rem(home + j, quarters) for j in nearest]
    for q in order:

        @pl.loop(2 * q, 2 * q + 2)
        def _(e):
            for i in range(per):
                z = e * per + i

                @pl.when(z != zi)
                def _():
                    remote(chunk(z, xi), chunk(z, xi), s3s.at[z], s3r.at[z], at()).wait_recv()

            for i in range(1, x_n):
                send4(lax.rem(xi + i, x_n), e).start()

    def turn_got(y):
        @pl.loop(0, zh_n)
        def _(h):
            for c in range(c_n):
                got_g(y * c_n + c, h).wait_recv()
            turn_slot(y, h)

    for j in near:
        turn_got(jnp.bitwise_xor(yi, j))

    for q in order:
        for e in (2 * q, 2 * q + 1):
            for i in range(1, x_n):
                x = lax.rem(xi + i, x_n)
                remote(block(e, x), block(e, x), s4s.at[x, e], s4r.at[x, e], at()).wait_recv()
        h = lax.div(2 * q, owners)
        these = lines_of(lax.rem(2 * q, owners), 2)
        product = jnp.dot(chosen[h, these, :], rot[h], preferred_element_type=F32)
        asked[h, these, :] = (product / divisor[h]).astype(BF16)

    def score(y):
        some = pl.ds(pl.multiple_of(y * c_n * rows, c_n * rows), c_n * rows)
        total = None
        for h in range(zh_n):
            term = lax.dot_general(
                turned[h, some, :], asked[h], (((1,), (1,)), ((), ())), preferred_element_type=F32
            )
            total = term if total is None else total + term
        part[pl.ds(y * c_n, c_n)] = total.reshape(c_n, rows, total.shape[1]).astype(BF16)
        return total

    def send_p(t):
        return remote(part.at[t], parts.at[ti], sps.at[t], spr.at[ti], at(t=t))

    for j in near + far + [0]:
        y = jnp.bitwise_xor(yi, j)
        if j in far:
            turn_got(y)
        total = score(y)
        for c in range(c_n):
            if j:
                send_p(y * c_n + c).start()
        if j == 0:
            send_p(sibling).start()
            whole[...] = total.reshape(c_n, rows, total.shape[1])

    @pl.loop(1, zl_n)
    def _(i):
        send2(lax.rem(zl + i, zl_n)).wait_send()

    @pl.loop(1, z_n)
    def _(i):
        send3(lax.rem(zi + i, z_n)).wait_send()

    @pl.loop(1, x_n)
    def _(i):
        x = lax.rem(xi + i, x_n)
        send1(x).wait_send()
        for e in range(blocks):
            send4(x, e).wait_send()

    @pl.loop(1, t_n)
    def _(i):
        for h in range(zh_n):
            send_g(jnp.bitwise_xor(ti, i), h).wait_send()

    @pl.loop(1, t_n)
    def _(i):
        t = jnp.bitwise_xor(ti, i)
        remote(parts.at[t], parts.at[t], sps.at[t], spr.at[t], at()).wait_recv()

    total = whole[lax.rem(ti, c_n)]
    for i in range(1, t_n):
        total += parts[jnp.bitwise_xor(ti, i)].astype(F32)
    out_ref[...] = total * (1.0 / math.sqrt(modules * width))

    @pl.loop(1, t_n)
    def _(i):
        send_p(jnp.bitwise_xor(ti, i)).wait_send()


def local(dims, train_grads, query_grads, basis_out, basis_in, eigenvalues, owner_groups, module_order):
    zl_n, x_n, zh_n, y_n, c_n = dims
    rows, modules, width = train_grads.shape
    held, side = query_grads.shape[1], basis_out.shape[1]
    t_n, z_n, owners = y_n * c_n, zh_n * zl_n, owner_groups.shape[0]
    asks, wide_x, piece = owners * held, width // x_n, width // x_n // (zl_n // owners)
    dma = pltpu.SemaphoreType.DMA
    return pl.pallas_call(
        functools.partial(kernel, dims),
        out_shape=jax.ShapeDtypeStruct((rows, asks), F32),
        in_specs=[pl.BlockSpec(memory_space=pl.ANY)] * 7,
        out_specs=pl.BlockSpec(memory_space=pltpu.VMEM),
        scratch_shapes=[
            pltpu.VMEM((rows, modules, width), BF16),
            pltpu.VMEM((held, width), BF16),
            pltpu.VMEM((side, side), BF16),
            pltpu.VMEM((side, side), BF16),
            pltpu.SMEM(owner_groups.shape, jnp.int32),
            pltpu.SMEM(module_order.shape, jnp.int32),
            dma((7,)),
            pltpu.VMEM((16 * modules, 16 * modules), BF16),
            pltpu.VMEM((modules, rows, width), BF16),
            pltpu.VMEM((zh_n, t_n * rows, width), BF16),
            pltpu.VMEM((zh_n, width, width), BF16),
            pltpu.VMEM((zh_n, t_n * rows, width), BF16),
            pltpu.VMEM((zh_n, side, 128), BF16),
            pltpu.VMEM((zh_n, 1, width), F32),
            pltpu.SemaphoreType.REGULAR((max(1, (z_n // 2).bit_length() - 2),)),
            pltpu.VMEM((x_n, held, wide_x), BF16),
            pltpu.VMEM((owners, held, wide_x), BF16),
            pltpu.VMEM((zl_n, held, piece), BF16),
            pltpu.VMEM((zh_n, asks, width), BF16),
            pltpu.VMEM((zh_n, asks, width), BF16),
            pltpu.VMEM((zh_n, 1, width), F32),
            pltpu.VMEM((t_n, rows, asks), BF16),
            pltpu.VMEM((t_n, rows, asks), BF16),
            pltpu.VMEM((c_n, rows, asks), F32),
            dma((x_n,)),
            dma((x_n,)),
            dma((zl_n,)),
            dma((zl_n,)),
            dma((z_n,)),
            dma((z_n,)),
            dma((x_n, zh_n * owners)),
            dma((x_n, zh_n * owners)),
            dma((t_n, zh_n)),
            dma((t_n, zh_n)),
            dma((2,)),
            dma((2,)),
            dma((t_n,)),
            dma((t_n,)),
        ],
        compiler_params=pltpu.CompilerParams(
            collective_id=0, has_side_effects=True, vmem_limit_bytes=60 << 20
        ),
    )(
        train_grads,
        query_grads.reshape(held, width),
        basis_out[0],
        basis_in[0],
        eigenvalues,
        owner_groups,
        module_order,
    )


def solution(mesh, layout=(X, ZH, Y, C)):
    x_n, zh_n, y_n, c_n = layout
    dims = (mesh.shape["group"] // x_n, x_n, zh_n, y_n, c_n)
    in_specs = (
        P(("group", "module"), None, None),
        P("group", None, "module", None),
        P("module", None, None),
        P("module", None, None),
        P("module", None),
        P(),
        P(),
    )
    out_specs = P(("group", "module"), None)
    return jax.shard_map(
        functools.partial(local, dims), mesh=mesh, in_specs=in_specs, out_specs=out_specs, check_vma=False
    )
```

```python
import functools
import math

import jax
import jax.numpy as jnp
from jax import lax
from jax.experimental import pallas as pl
from jax.experimental.pallas import tpu as pltpu
from jax.sharding import PartitionSpec as P

ZH, Y, C = 2, 4, 2
X = 4
F32, BF16 = jnp.float32, jnp.bfloat16


def kernel(
    dims,
    train_hbm,
    query_hbm,
    bout_hbm,
    bin_hbm,
    eig_hbm,
    owner_hbm,
    order_hbm,
    out_ref,
    train_ref,
    query_ref,
    bout_ref,
    bin_ref,
    owner_ref,
    order_ref,
    fetch_sem,
    perm,
    ordered,
    gathered,
    rot,
    turned,
    bases,
    eigs,
    heard,
    crossed,
    offer,
    offered,
    chosen,
    asked,
    divisor,
    part,
    parts,
    whole,
    s1s,
    s1r,
    s2s,
    s2r,
    s3s,
    s3r,
    s4s,
    s4r,
    sgs,
    sgr,
    sbs,
    sbr,
    sps,
    spr,
):
    zl_n, x_n, zh_n, y_n, c_n = dims
    t_n = y_n * c_n
    z_n = zh_n * zl_n
    rows, modules, width = train_ref.shape
    held = query_ref.shape[0]
    owners = owner_hbm.shape[0]
    per = zl_n // owners
    wide_x = width // x_n
    piece = wide_x // per
    group, module = lax.axis_index("group"), lax.axis_index("module")
    zl, xi = lax.div(group, x_n), lax.rem(group, x_n)
    zh, ti = lax.div(module, t_n), lax.rem(module, t_n)
    yi = lax.div(ti, c_n)
    zi = zh * zl_n + zl

    def at(z=None, x=None, t=None):
        z = zi if z is None else z
        x = xi if x is None else x
        t = ti if t is None else t
        return (lax.rem(z, zl_n) * x_n + x, lax.div(z, zl_n) * t_n + t)

    def remote(src, dst, send, recv, where):
        return pltpu.make_async_remote_copy(
            src_ref=src,
            dst_ref=dst,
            send_sem=send,
            recv_sem=recv,
            device_id=where,
            device_id_type=pl.DeviceIdType.MESH,
        )

    fetches = [
        pltpu.make_async_copy(src, dst, fetch_sem.at[i])
        for i, (src, dst) in enumerate(
            (
                (order_hbm, order_ref),
                (train_hbm, train_ref),
                (query_hbm, query_ref),
                (bout_hbm, bout_ref),
                (bin_hbm, bin_ref),
                (eig_hbm, eigs.at[zh]),
                (owner_hbm, owner_ref),
            )
        )
    ]
    for fetch in fetches:
        fetch.start()

    barrier = pltpu.get_barrier_semaphore()

    def greet(where):
        pl.semaphore_signal(
            barrier, inc=1, device_id=where, device_id_type=pl.DeviceIdType.MESH
        )

    around = sorted({1, 2, z_n - 2, z_n - 1})
    for i in around:
        greet(at(z=lax.rem(zi + i, z_n)))

    @pl.loop(1, x_n)
    def _(i):
        greet(at(x=lax.rem(xi + i, x_n)))

    @pl.loop(1, t_n)
    def _(i):
        greet(at(t=lax.rem(ti + i, t_n)))

    order_in, train_in, query_in, *small_in = fetches

    batch = 16
    span = batch * modules
    order_in.wait()
    for s in range(modules):
        lane = lax.broadcasted_iota(jnp.int32, (batch, span), 1)
        row = lax.broadcasted_iota(jnp.int32, (batch, span), 0)
        hit = lane == row * modules + order_ref[s]
        perm[pl.ds(s * batch, batch), :] = jnp.where(hit, 1.0, 0.0).astype(BF16)
    train_in.wait()
    for b in range(rows // batch):
        block = train_ref[pl.ds(b * batch, batch)].reshape(span, width)
        moved = jnp.dot(perm[...], block, preferred_element_type=F32).astype(BF16)
        ordered[:, pl.ds(b * batch, batch), :] = moved.reshape(modules, batch, width)
    query_in.wait()
    pl.semaphore_wait(barrier, len(around) + x_n + t_n - 2)

    def columns_of(x):
        return pl.ds(pl.multiple_of(x * wide_x, wide_x), wide_x)

    def send1(x):
        return remote(
            query_ref.at[:, columns_of(x)], crossed.at[xi], s1s.at[x], s1r.at[xi], at(x=x)
        )

    @pl.loop(1, x_n)
    def _(i):
        send1(lax.rem(xi + i, x_n)).start()

    def tell(step):
        d = 2 << step
        for z in (lax.rem(zi + d, z_n), lax.rem(zi + z_n - d, z_n)):
            pl.semaphore_signal(
                heard.at[step], inc=1, device_id=at(z=z), device_id_type=pl.DeviceIdType.MESH
            )

    def hear(step):
        pl.semaphore_wait(heard.at[step], 2)
        if step + 1 < steps:
            tell(step + 1)

    steps = (z_n // 2).bit_length() - 2
    if steps:
        tell(0)

    def send_g(t, h):
        return remote(
            ordered.at[h * t_n + t],
            gathered.at[h, pl.ds(pl.multiple_of(ti * rows, rows), rows)],
            sgs.at[t, h],
            sgr.at[ti, h],
            at(t=t),
        )

    def got_g(t, h):
        return remote(
            ordered.at[h * t_n + t],
            gathered.at[h, pl.ds(pl.multiple_of(t * rows, rows), rows)],
            sgs.at[t, h],
            sgr.at[t, h],
            at(t=t),
        )

    near = [j for j in range(1, y_n) if j != 2]
    far = [j for j in range(1, y_n) if j == 2]
    for j in [0] + near + far:
        for h in range(zh_n):
            for c in range(1 if j == 0 else 0, c_n):
                send_g(jnp.bitwise_xor(ti, j * c_n + c), h).start()

    if steps:
        hear(0)
    for fetch in small_in:
        fetch.wait()

    bases[zh] = jnp.zeros(bases.shape[1:], BF16)
    side = bout_ref.shape[1]
    bases[zh, :, :side] = bout_ref[...]
    bases[zh, :, side : 2 * side] = bin_ref[...]

    def build(h):
        lane = lax.broadcasted_iota(jnp.int32, (bases.shape[2], width), 1)
        row = lax.broadcasted_iota(jnp.int32, (bases.shape[2], width), 0)
        wide = jnp.where(lax.div(lane, side) == row, 1.0, 0.0).astype(BF16)
        tiled = jnp.where(lax.rem(lane, side) + side == row, 1.0, 0.0).astype(BF16)
        outer = jnp.dot(bases[h], wide, preferred_element_type=F32)
        inner = jnp.dot(bases[h], tiled, preferred_element_type=F32)
        for a in range(side):
            rot[h, pl.ds(a * side, side), :] = (outer[a : a + 1] * inner).astype(BF16)

    build(zh)

    for h in range(zh_n):
        gathered[h, pl.ds(pl.multiple_of(ti * rows, rows), rows)] = ordered[h * t_n + ti]

    crossed[xi] = query_ref[:, columns_of(xi)]

    @pl.loop(1, x_n)
    def _(i):
        x = lax.rem(xi + i, x_n)
        remote(crossed.at[x], crossed.at[x], s1s.at[x], s1r.at[x], at()).wait_recv()

    for k in range(owners):
        offer[k] = crossed[lax.rem(owner_ref[k], x_n)]
    for step in range(1, steps):
        hear(step)

    def lines_of(k, n=1):
        return pl.ds(pl.multiple_of(k * held, n * held), n * held)

    def send2(z):
        part_z = pl.ds(pl.multiple_of(lax.rem(z, per) * piece, piece), piece)
        return remote(
            offer.at[lax.div(z, per), :, part_z],
            offered.at[zl],
            s2s.at[z],
            s2r.at[zl],
            at(z=zh * zl_n + z),
        )

    @pl.loop(1, zl_n)
    def _(i):
        send2(lax.rem(zl + i, zl_n)).start()

    other = zh_n - 1 - zh
    twins = [
        remote(bases.at[zh], bases.at[zh], sbs.at[0], sbr.at[0], at(z=z_n - 1 - zi)),
        remote(eigs.at[zh], eigs.at[zh], sbs.at[1], sbr.at[1], at(z=z_n - 1 - zi)),
    ]
    for twin in twins:
        twin.start()

    mine = lax.div(zl, per)
    offered[zl] = offer[mine, :, pl.ds(pl.multiple_of(lax.rem(zl, per) * piece, piece), piece)]

    @pl.loop(1, zl_n)
    def _(i):
        z = lax.rem(zl + i, zl_n)
        remote(offered.at[z], offered.at[z], s2s.at[z], s2r.at[z], at()).wait_recv()

    def place(z, x):
        zz = lax.rem(z, zl_n)
        start = x * wide_x + lax.rem(zz, per) * piece
        return (
            lax.div(z, zl_n),
            lines_of(lax.div(zz, per)),
            pl.ds(pl.multiple_of(start, piece), piece),
        )

    def chunk(z, x):
        return chosen.at[place(z, x)]

    chosen[place(zi, xi)] = offered[lax.div(owner_ref[mine], x_n)]

    def send3(z):
        return remote(chunk(zi, xi), chunk(zi, xi), s3s.at[z], s3r.at[zi], at(z=z))

    send3(lax.rem(zi + z_n // 2, z_n)).start()

    @pl.loop(1, z_n // 2)
    def _(i):
        send3(lax.rem(zi + z_n // 2 - i, z_n)).start()
        send3(lax.rem(zi + z_n // 2 + i, z_n)).start()

    for twin in twins:
        twin.wait_send()
    for i, buf in enumerate((bases, eigs)):
        remote(buf.at[other], buf.at[other], sbs.at[i], sbr.at[i], at()).wait_recv()
    build(other)

    def turn_slot(y, h):
        some = pl.ds(pl.multiple_of(y * c_n * rows, c_n * rows), c_n * rows)
        turned[h, some, :] = jnp.dot(
            gathered[h, some, :], rot[h], preferred_element_type=F32
        ).astype(BF16)

    sibling = jnp.bitwise_xor(ti, 1)
    for h in range(zh_n):
        divisor[h] = eigs[h] + 0.1 * jnp.mean(eigs[h], axis=1, keepdims=True)

    def block(e, x):
        return chosen.at[lax.div(e, owners), lines_of(lax.rem(e, owners)), columns_of(x)]

    def send4(x, e):
        return remote(block(e, xi), block(e, xi), s4s.at[x, e], s4r.at[xi, e], at(x=x))

    blocks = s4s.shape[1]
    quarters = blocks // 2
    home = lax.div(zi, 2 * per)
    nearest = (2, 1, 3, 0) if quarters == 4 else range(quarters)
    order = [lax.rem(home + j, quarters) for j in nearest]
    for q in order:

        @pl.loop(2 * q, 2 * q + 2)
        def _(e):
            for i in range(per):
                z = e * per + i

                @pl.when(z != zi)
                def _():
                    remote(chunk(z, xi), chunk(z, xi), s3s.at[z], s3r.at[z], at()).wait_recv()

            for i in range(1, x_n):
                send4(lax.rem(xi + i, x_n), e).start()

    for h in range(zh_n):
        got_g(sibling, h).wait_recv()

    @pl.loop(0, zh_n)
    def _(h):
        turn_slot(yi, h)

    def turn_got(y):
        @pl.loop(0, zh_n)
        def _(h):
            for c in range(c_n):
                got_g(y * c_n + c, h).wait_recv()
            turn_slot(y, h)

    for j in near:
        turn_got(jnp.bitwise_xor(yi, j))

    for q in order:
        for e in (2 * q, 2 * q + 1):
            for i in range(1, x_n):
                x = lax.rem(xi + i, x_n)
                remote(block(e, x), block(e, x), s4s.at[x, e], s4r.at[x, e], at()).wait_recv()
        h = lax.div(2 * q, owners)
        these = lines_of(lax.rem(2 * q, owners), 2)
        product = jnp.dot(chosen[h, these, :], rot[h], preferred_element_type=F32)
        asked[h, these, :] = (product / divisor[h]).astype(BF16)

    def score(y):
        some = pl.ds(pl.multiple_of(y * c_n * rows, c_n * rows), c_n * rows)
        total = None
        for h in range(zh_n):
            term = lax.dot_general(
                turned[h, some, :], asked[h], (((1,), (1,)), ((), ())), preferred_element_type=F32
            )
            total = term if total is None else total + term
        part[pl.ds(y * c_n, c_n)] = total.reshape(c_n, rows, total.shape[1]).astype(BF16)
        return total

    def send_p(t):
        return remote(part.at[t], parts.at[ti], sps.at[t], spr.at[ti], at(t=t))

    for j in near + far + [0]:
        y = jnp.bitwise_xor(yi, j)
        if j in far:
            turn_got(y)
        total = score(y)
        for c in range(c_n):
            if j:
                send_p(y * c_n + c).start()
        if j == 0:
            send_p(sibling).start()
            whole[...] = total.reshape(c_n, rows, total.shape[1])

    @pl.loop(1, zl_n)
    def _(i):
        send2(lax.rem(zl + i, zl_n)).wait_send()

    @pl.loop(1, z_n)
    def _(i):
        send3(lax.rem(zi + i, z_n)).wait_send()

    @pl.loop(1, x_n)
    def _(i):
        x = lax.rem(xi + i, x_n)
        send1(x).wait_send()
        for e in range(blocks):
            send4(x, e).wait_send()

    @pl.loop(1, t_n)
    def _(i):
        for h in range(zh_n):
            send_g(jnp.bitwise_xor(ti, i), h).wait_send()

    @pl.loop(1, t_n)
    def _(i):
        t = jnp.bitwise_xor(ti, i)
        remote(parts.at[t], parts.at[t], sps.at[t], spr.at[t], at()).wait_recv()

    total = whole[lax.rem(ti, c_n)]
    for i in range(1, t_n):
        total += parts[jnp.bitwise_xor(ti, i)].astype(F32)
    out_ref[...] = total * (1.0 / math.sqrt(modules * width))

    @pl.loop(1, t_n)
    def _(i):
        send_p(jnp.bitwise_xor(ti, i)).wait_send()


def local(dims, train_grads, query_grads, basis_out, basis_in, eigenvalues, owner_groups, module_order):
    zl_n, x_n, zh_n, y_n, c_n = dims
    rows, modules, width = train_grads.shape
    held, side = query_grads.shape[1], basis_out.shape[1]
    t_n, z_n, owners = y_n * c_n, zh_n * zl_n, owner_groups.shape[0]
    asks, wide_x, piece = owners * held, width // x_n, width // x_n // (zl_n // owners)
    dma = pltpu.SemaphoreType.DMA
    return pl.pallas_call(
        functools.partial(kernel, dims),
        out_shape=jax.ShapeDtypeStruct((rows, asks), F32),
        in_specs=[pl.BlockSpec(memory_space=pl.ANY)] * 7,
        out_specs=pl.BlockSpec(memory_space=pltpu.VMEM),
        scratch_shapes=[
            pltpu.VMEM((rows, modules, width), BF16),
            pltpu.VMEM((held, width), BF16),
            pltpu.VMEM((side, side), BF16),
            pltpu.VMEM((side, side), BF16),
            pltpu.SMEM(owner_groups.shape, jnp.int32),
            pltpu.SMEM(module_order.shape, jnp.int32),
            dma((7,)),
            pltpu.VMEM((16 * modules, 16 * modules), BF16),
            pltpu.VMEM((modules, rows, width), BF16),
            pltpu.VMEM((zh_n, t_n * rows, width), BF16),
            pltpu.VMEM((zh_n, width, width), BF16),
            pltpu.VMEM((zh_n, t_n * rows, width), BF16),
            pltpu.VMEM((zh_n, side, 128), BF16),
            pltpu.VMEM((zh_n, 1, width), F32),
            pltpu.SemaphoreType.REGULAR((max(1, (z_n // 2).bit_length() - 2),)),
            pltpu.VMEM((x_n, held, wide_x), BF16),
            pltpu.VMEM((owners, held, wide_x), BF16),
            pltpu.VMEM((zl_n, held, piece), BF16),
            pltpu.VMEM((zh_n, asks, width), BF16),
            pltpu.VMEM((zh_n, asks, width), BF16),
            pltpu.VMEM((zh_n, 1, width), F32),
            pltpu.VMEM((t_n, rows, asks), BF16),
            pltpu.VMEM((t_n, rows, asks), BF16),
            pltpu.VMEM((c_n, rows, asks), F32),
            dma((x_n,)),
            dma((x_n,)),
            dma((zl_n,)),
            dma((zl_n,)),
            dma((z_n,)),
            dma((z_n,)),
            dma((x_n, zh_n * owners)),
            dma((x_n, zh_n * owners)),
            dma((t_n, zh_n)),
            dma((t_n, zh_n)),
            dma((2,)),
            dma((2,)),
            dma((t_n,)),
            dma((t_n,)),
        ],
        compiler_params=pltpu.CompilerParams(
            collective_id=0, has_side_effects=True, vmem_limit_bytes=60 << 20
        ),
    )(
        train_grads,
        query_grads.reshape(held, width),
        basis_out[0],
        basis_in[0],
        eigenvalues,
        owner_groups,
        module_order,
    )


def solution(mesh, layout=(X, ZH, Y, C)):
    x_n, zh_n, y_n, c_n = layout
    dims = (mesh.shape["group"] // x_n, x_n, zh_n, y_n, c_n)
    in_specs = (
        P(("group", "module"), None, None),
        P("group", None, "module", None),
        P("module", None, None),
        P("module", None, None),
        P("module", None),
        P(),
        P(),
    )
    out_specs = P(("group", "module"), None)
    return jax.shard_map(
        functools.partial(local, dims), mesh=mesh, in_specs=in_specs, out_specs=out_specs, check_vma=False
    )
```
